128 devices in a mesh: wide: 16 (over z, x), narrow: 8 (over y, core).
Axes of the slice: x: 4, y: 4, z: 4, core: 2. Of those that a mesh axis runs over, the one named last changes fastest.
Arguments:
- charges: bfloat16 [64, 524288], P(None, ('wide', 'narrow')), may hold values from -6 to 6
- basis: bfloat16 [64, 524288], P(None, ('wide', 'narrow')), may hold values from -0.75 to 0.75
- transfer: bfloat16 [4096, 8192], P(('wide', 'narrow')), may hold values from -0.5 to 0.5
- coupling: bfloat16 [12288, 98304], P(('wide', 'narrow')), may hold values from -0.15625 to 0.15625
- near_blocks: bfloat16 [8192, 20480], P(('wide', 'narrow')), may hold values from -0.3125 to 0.3125
- local_slot: int32 [12288, 20], P(('wide', 'narrow')), may hold values from 0 to 63, as said below
- owner: int32 [12288, 4], P(('wide', 'narrow')), may hold values from 0 to 127, all different within a row; in each aligned block of 32 rows (0 to 31, 32 to 63, ...) at most 2 rows name the same one
- far_slot: int32 [12288, 4], P(('wide', 'narrow')), may hold values from 0 to 63, as said below
Outputs:
- potential: float32 [64, 524288], P(None, ('wide', 'narrow'))
The draws below stay inside these ranges and needn't reach their ends.
Inputs may be any that keep to these rules, and one draw needn't show every extreme that they name: `owner`: in every row the 4 entries name different devices. In every aligned block of 32 rows no device is named more than 2 times, and some device exactly 2 times. `local_slot`: below 64 in rows of leaves and below 32 in rows of parents. `far_slot`: below 64 in rows of leaves and below 32 in rows of parents.
All inputs are finite; a program needn't handle non-finite values.
Results may differ from the reference program's by a relative error of at most 0.004.
Values may be sent and summed in bfloat16 or wider, within the bound.
A program may use at most 320 MiB of HBM per device.

```python
import math
import jax
import jax.numpy as jnp
import numpy as np
from jax import lax

LEAF = 64
RANK = 64
RHS = 64
K_LOCAL = 20
K_FAR = 4
REACH = 2
LEAF_DEV = 64
BLOCK = 32
NODES_DEV = 96
MOST = 2
LEAVES = 8192
PARENTS = 4096
NODES = 12288
POINTS = 524288
DEVICES = 128


def level_sizes():
    rows_local = jnp.arange(NODES, dtype=jnp.int32) % NODES_DEV
    return jnp.where(rows_local < LEAF_DEV, LEAF_DEV, BLOCK).astype(jnp.int32)


def draw_local_slot(key, part):
    key = jax.random.fold_in(key, 11)
    raw_values = jax.random.randint(key, (NODES, K_LOCAL), 0, 2 ** 30, dtype=jnp.int32)
    values = raw_values % level_sizes()[:, None]
    return values.at[0, 0].set(LEAF_DEV - 1).at[1, 0].set(0)


def draw_far_slot(key, part):
    key = jax.random.fold_in(key, 23)
    raw_values = jax.random.randint(key, (NODES, K_FAR), 0, 2 ** 30, dtype=jnp.int32)
    values = raw_values % level_sizes()[:, None]
    return values.at[0, 0].set(LEAF_DEV - 1).at[1, 0].set(0)


def block_scale(own_key, shape, cuts, least, largest):
    factor_of, own = 1.0, jax.random.fold_in(own_key, 6)
    for axis_at, shards_of in cuts:
        steps = jnp.exp(jax.random.uniform(jax.random.fold_in(own, axis_at), (shards_of,), jnp.float32, least / len(cuts), largest / len(cuts)))
        factor_of = factor_of * jnp.repeat(steps, shape[axis_at] // shards_of).reshape([-1 if axis == axis_at else 1 for axis in range(len(shape))])
    return factor_of


def assign_block(own_key, own, number, rows, count, top, most, skew):
    sequence = jax.random.permutation(own_key, count)
    heavy_load, common = portions_of(count, rows * top, most, skew, True), portions_of(count, rows * top, most, skew, False)
    places = jnp.arange(count)

    def named(tallies, rotation):
        used = int((tallies > 0).sum())
        fixed = max(1, used // 4)
        moved = fixed + (places - fixed + rotation * (used - fixed)) % max(1, count - fixed)
        return jnp.zeros((count,), jnp.int32).at[sequence[jnp.where(places < fixed, places, moved)]].set(jnp.asarray(tallies, jnp.int32))

    tallies = jnp.where(number % 4 == 0, named(heavy_load, number // 4), named(common, number - number // 4 - 1))
    mixed = jax.random.permutation(jax.random.fold_in(own, 3), count)
    giver, taker = mixed[0:count // 2 * 2:2], mixed[1:count // 2 * 2:2]
    slack = jnp.minimum(tallies[giver] - 1, most - tallies[taker]) // 2
    slack = jnp.where((giver == sequence[0]) | (taker == sequence[0]) | (tallies[taker] == 0), 0, jnp.maximum(slack, 0))
    moved = jax.random.randint(jax.random.fold_in(own, 4), (count // 2,), 0, 1 << 20) % (slack + 1)
    tallies = tallies.at[giver].add(-moved).at[taker].add(moved)
    members = jnp.searchsorted(jnp.cumsum(tallies), jnp.arange(rows * top), side="right").astype(jnp.int32)
    listing = members.reshape(top, rows).T
    listing = listing[jax.random.permutation(jax.random.fold_in(own, 1), rows)]
    rotation = jax.random.randint(jax.random.fold_in(own, 2), (rows, 1), 0, top)
    return jnp.take_along_axis(listing, (jnp.arange(top)[None, :] + rotation) % top, axis=1)


def portions_of(number_of, total, reach, lean, full):
    weights = [(1 << 20) // math.isqrt(rank ** lean) + 1 for rank in range(1, number_of + 1)]
    largest = reach if full else min(reach, max(-(-total // number_of), total * weights[0] // sum(weights)))
    least = 1 if total - largest >= number_of - 1 else 0
    given, spare = [largest] + [least] * (number_of - 1), total - largest - least * (number_of - 1)
    while spare > 0:
        movable = [i for i in range(1, number_of) if given[i] < largest] or [i for i in range(1, number_of) if given[i] < reach]
        pool, left = sum([weights[i] for i in movable]), spare
        for i in movable:
            more = min(reach - given[i], max(1, left * weights[i] // pool), spare)
            given[i] = given[i] + more
            spare = spare - more
    return np.array(given)


def gaussian(own_key, extent, deviation, bound, pieces=(), kind=jnp.bfloat16):
    loudness = block_scale(own_key, extent, pieces, -0.22, 0.18) if pieces else 1.0
    values = jax.random.normal(own_key, extent, jnp.float32) * deviation * loudness
    return jnp.minimum(jnp.maximum(values, -bound), bound).astype(kind)


def setup_inputs(seed: int = 0) -> dict:
    arg_keys = jax.random.split(jax.random.key(seed), 9)
    charges = gaussian(arg_keys[0], (RHS, POINTS), 1.0, 6.0, ((1, 128),))
    basis = gaussian(arg_keys[1], (RANK, POINTS), LEAF ** -0.5, 0.75, ((1, 128),))
    transfer = gaussian(arg_keys[2], (PARENTS, 2 * RANK * RANK), (2 * RANK) ** -0.5, 0.5, ((0, 128),))
    coupling = gaussian(arg_keys[3], (NODES, (K_LOCAL + K_FAR) * RANK * RANK), ((K_LOCAL + K_FAR) * RANK) ** -0.5, 0.15625, ((0, 128),))
    near_blocks = gaussian(arg_keys[4], (LEAVES, (2 * REACH + 1) * LEAF * LEAF), ((2 * REACH + 1) * LEAF) ** -0.5, 0.3125, ((0, 128),))
    local_slot = draw_local_slot(jax.random.fold_in(arg_keys[8], 71), 0)
    owner_keys = jax.random.split(jax.random.fold_in(arg_keys[6], 1), NODES // BLOCK)
    owner_turns = jax.random.permutation(jax.random.fold_in(arg_keys[6], 3), NODES // BLOCK)
    owner = jax.vmap(lambda own, number: assign_block(jax.random.fold_in(arg_keys[6], 2), own, number, BLOCK, DEVICES, K_FAR, MOST, 2))(owner_keys, owner_turns).reshape((NODES, K_FAR))
    far_slot = draw_far_slot(jax.random.fold_in(arg_keys[8], 71), 0)
    return {"charges": charges, "basis": basis, "transfer": transfer, "coupling": coupling, "near_blocks": near_blocks, "local_slot": local_slot, "owner": owner, "far_slot": far_slot}


def reference(charges, basis, transfer, coupling, near_blocks, local_slot, owner, far_slot):
    charge_cells = charges.astype(jnp.float32).reshape(RHS, LEAVES, LEAF)
    leaf_basis = basis.astype(jnp.float32).reshape(RANK, LEAVES, LEAF)
    leaf_coef = jnp.einsum('klp,rlp->lkr', leaf_basis, charge_cells).astype(jnp.bfloat16)
    leaf_coef = lax.optimization_barrier(leaf_coef)
    transfers = transfer.astype(jnp.float32).reshape(PARENTS, 2, RANK, RANK)
    children = leaf_coef.astype(jnp.float32).reshape(PARENTS, 2, RANK, RHS)
    parent_coef = jnp.einsum('pbjk,pbjr->pkr', transfers, children).astype(jnp.bfloat16)
    parent_coef = lax.optimization_barrier(parent_coef)
    stacked = jnp.concatenate([leaf_coef.reshape(DEVICES, LEAF_DEV, RANK, RHS),
                               parent_coef.reshape(DEVICES, BLOCK, RANK, RHS)], axis=1)
    offset = jnp.where(jnp.arange(NODES_DEV) < LEAF_DEV, 0, LEAF_DEV).astype(jnp.int32)
    slots_all = K_LOCAL + K_FAR
    coupling_tiles = coupling.reshape(DEVICES, NODES_DEV, slots_all, RANK, RANK)
    near_index = local_slot.reshape(DEVICES, NODES_DEV, K_LOCAL) + offset[None, :, None]
    far_device = owner.reshape(DEVICES, NODES_DEV, K_FAR)
    far_index = far_slot.reshape(DEVICES, NODES_DEV, K_FAR) + offset[None, :, None]

    def one_device(device_item):
        device_id, tiles, near_rows, far_dev, far_rows = device_item
        mine = jnp.take(stacked, device_id, axis=0)
        partners = jnp.concatenate([mine[near_rows], stacked[far_dev, far_rows]], axis=1).astype(jnp.float32)
        return jnp.einsum('nkij,nkjr->nir', tiles.astype(jnp.float32), partners)

    coupled = lax.map(one_device, (jnp.arange(DEVICES, dtype=jnp.int32), coupling_tiles,
                                   near_index, far_device, far_index))
    leaf_field = coupled[:, :LEAF_DEV].reshape(PARENTS, 2, RANK, RHS)
    parent_down = coupled[:, LEAF_DEV:].reshape(PARENTS, RANK, RHS).astype(jnp.bfloat16)
    parent_down = lax.optimization_barrier(parent_down)
    leaf_down = (leaf_field + jnp.einsum('pbjk,pkr->pbjr', transfers, parent_down.astype(jnp.float32))).astype(jnp.bfloat16)
    leaf_down = lax.optimization_barrier(leaf_down)
    far_part = jnp.einsum('klp,lkr->rlp', leaf_basis, leaf_down.astype(jnp.float32).reshape(LEAVES, RANK, RHS))
    padded = jnp.pad(charge_cells, ((0, 0), (REACH, REACH), (0, 0)))
    near_width = 2 * REACH + 1
    near_tiles = near_blocks.astype(jnp.float32).reshape(LEAVES, near_width, LEAF, LEAF)
    near_part = jnp.zeros_like(far_part)
    for step in range(near_width):
        near_part = near_part + jnp.einsum('lps,rls->rlp', near_tiles[:, step], padded[:, step:step + LEAVES])
    return (far_part + near_part).reshape(RHS, POINTS)
```

```python
import functools

import jax
import jax.numpy as jnp
from jax import lax
from jax.experimental import pallas as pl
from jax.experimental.pallas import tpu as pltpu
from jax.sharding import PartitionSpec as P

MESH = pl.DeviceIdType.MESH
F32, BF16, I32 = jnp.float32, jnp.bfloat16, jnp.int32

WIDE, NARROW = 16, 8
LEAF_DEV, PARENTS, NODES = 64, 32, 96
K_LOCAL, K_FAR = 20, 4
ENTRIES = NODES * K_FAR
CAP = 48
VMEM_LIMIT = 56 << 20


def lo_mask(rows):
    return lax.broadcasted_iota(I32, (rows, 128), 1) < 64


def swap_halves(x):
    return jnp.concatenate([x[:, 64:], x[:, :64]], axis=1)


def mm(a, b, dims=((1,), (0,))):
    return lax.dot_general(a, b, (dims, ((), ())), preferred_element_type=F32)


def spread(tile):
    lo = lo_mask(32)
    zero = jnp.zeros_like(tile)
    turned = swap_halves(tile)
    return jnp.concatenate(
        [
            jnp.where(lo, tile, zero),
            jnp.where(lo, turned, zero),
            jnp.where(lo, zero, turned),
            jnp.where(lo, zero, tile),
        ],
        axis=0,
    )


def unpair(ref, start, packed):
    lo = lo_mask(32)
    turned = swap_halves(packed)
    ref[pl.ds(start, 32, stride=2), :] = jnp.where(lo, packed, turned)
    ref[pl.ds(start + 1, 32, stride=2), :] = jnp.where(lo, turned, packed)


def to_rows(src, dst, tiles, rows):
    def step(g, c):
        for u in range(8):
            t = g * 8 + u
            dst[pl.ds(pl.multiple_of(t * rows, rows), rows), :] = src[
                :, pl.ds(pl.multiple_of(t * 128, 128), 128)
            ].astype(F32)
        return c

    lax.fori_loop(0, tiles // 8, step, 0)


def coef_kernel(charges, basis, transfer, out, rows, v):
    to_rows(transfer, rows, 64, PARENTS)
    lo64, lo32 = lo_mask(64), lo_mask(32)

    def step(p, c):
        cols = pl.ds(pl.multiple_of(p * 128, 128), 128)
        b, q = basis[:, cols], charges[:, cols]
        zero = jnp.zeros_like(b)
        bb = jnp.concatenate([jnp.where(lo64, b, zero), jnp.where(lo64, zero, b)], axis=0)
        qq = jnp.concatenate([q, q], axis=0)
        leaf = mm(bb, qq, ((1,), (1,))).astype(BF16)
        out[2 * p] = jnp.where(lo32, leaf[0:32], leaf[32:64])
        out[2 * p + 1] = jnp.where(lo32, leaf[64:96], leaf[96:128])
        v[...] = leaf.astype(F32)
        even, odd = v[pl.ds(0, 64, stride=2), :], v[pl.ds(1, 64, stride=2), :]
        paired = jnp.where(lo64, even, odd).astype(BF16)
        a = rows[pl.ds(p, 64, stride=PARENTS), :].astype(BF16)
        m = mm(a, paired, ((0,), (0,)))
        s = jnp.where(lo64, m[0:64], m[64:128])
        parent = (s + swap_halves(s)).astype(BF16)
        out[LEAF_DEV + p] = jnp.where(lo32, parent[0:32], parent[32:64])
        return c

    lax.fori_loop(0, PARENTS, step, 0)


def coefs(charges, basis, transfer):
    return pl.pallas_call(
        coef_kernel,
        out_shape=jax.ShapeDtypeStruct((NODES, 32, 128), BF16),
        in_specs=[pl.BlockSpec(memory_space=pltpu.VMEM)] * 3,
        out_specs=pl.BlockSpec(memory_space=pltpu.VMEM),
        scratch_shapes=[pltpu.VMEM((64 * PARENTS, 128), F32), pltpu.VMEM((128, 128), F32)],
        compiler_params=pltpu.CompilerParams(vmem_limit_bytes=VMEM_LIMIT),
        name="coefs",
    )(charges, basis, transfer)


def gather_kernel(x_ref, t_ref, q_ref, o_ref, ot_ref, oh_ref, ss, rs, ts, tr, hs, hr):
    w, n = lax.axis_index("wide"), lax.axis_index("narrow")
    y, c = n // 2, n % 2
    up, dn = lax.rem(y + 1, 4) * 2 + c, lax.rem(y + 3, 4) * 2 + c
    co, op = y * 2 + 1 - c, lax.rem(y + 2, 4) * 2 + c
    me = w * NARROW + n
    nxt, prv = lax.rem(me + 1, 128), lax.rem(me + 127, 128)
    bar = pltpu.get_barrier_semaphore()
    z, x = w // 4, w % 4
    peers = [
        lax.rem(z + dz, 4) * 4 + lax.rem(x + dx, 4)
        for dz in range(4)
        for dx in range(4)
        if dz or dx
    ]
    for p in (up, dn, co):
        pl.semaphore_signal(bar, inc=1, device_id=(w, p), device_id_type=MESH)
    for p in (nxt, prv):
        pl.semaphore_signal(bar, inc=1, device_id=(p // NARROW, p % NARROW), device_id_type=MESH)
    for p in peers:
        pl.semaphore_signal(bar, inc=1, device_id=(p, n), device_id_type=MESH)
    pl.semaphore_wait(bar, 20)

    copies = []

    def send(src, dst, ssem, rsem, dev):
        k = pltpu.make_async_remote_copy(
            src_ref=src, dst_ref=dst, send_sem=ssem, recv_sem=rsem, device_id=dev, device_id_type=MESH
        )
        k.start()
        copies.append(k)
        return k

    for i, p in enumerate(peers):
        send(t_ref, ot_ref.at[w], ts.at[i], tr.at[i], (p, n))
    h0 = send(q_ref.at[:, pl.ds(3968, 128)], oh_ref.at[0], hs.at[0], hr.at[0], (nxt // NARROW, nxt % NARROW))
    h1 = send(q_ref.at[:, pl.ds(0, 128)], oh_ref.at[1], hs.at[1], hr.at[1], (prv // NARROW, prv % NARROW))
    half = NODES // 2
    k0 = send(x_ref, o_ref.at[n], ss.at[0], rs.at[0], (w, up))
    k1 = send(x_ref, o_ref.at[n], ss.at[1], rs.at[1], (w, dn))
    k2 = send(x_ref, o_ref.at[n], ss.at[2], rs.at[2], (w, co))
    o_ref[n] = x_ref[...]
    ot_ref[w] = t_ref[...]
    k0.wait_recv()
    k3 = send(o_ref.at[dn, pl.ds(0, half)], o_ref.at[dn, pl.ds(0, half)], ss.at[3], rs.at[3], (w, up))
    k4 = send(o_ref.at[dn], o_ref.at[dn], ss.at[4], rs.at[4], (w, co))
    k1.wait_recv()
    k5 = send(o_ref.at[up, pl.ds(half, half)], o_ref.at[up, pl.ds(half, half)], ss.at[5], rs.at[5], (w, dn))
    k6 = send(o_ref.at[up], o_ref.at[up], ss.at[6], rs.at[6], (w, co))
    k3.wait_recv()
    k5.wait_recv()
    k7 = send(o_ref.at[op], o_ref.at[op], ss.at[7], rs.at[7], (w, co))
    for k in (k2, k4, k6, k7):
        k.wait_recv()
    for k in copies[:17]:
        k.wait_recv()
    for k in copies:
        k.wait_send()


def gather(x, table, charges):
    vm = pl.BlockSpec(memory_space=pltpu.VMEM)
    return pl.pallas_call(
        gather_kernel,
        out_shape=(
            jax.ShapeDtypeStruct((NARROW, NODES, 32, 128), BF16),
            jax.ShapeDtypeStruct((WIDE, 8, 128), I32),
            jax.ShapeDtypeStruct((2, 64, 128), BF16),
        ),
        in_specs=[vm] * 3,
        out_specs=(vm, vm, vm),
        scratch_shapes=[
            pltpu.SemaphoreType.DMA((8,)),
            pltpu.SemaphoreType.DMA((8,)),
            pltpu.SemaphoreType.DMA((15,)),
            pltpu.SemaphoreType.DMA((15,)),
            pltpu.SemaphoreType.DMA((2,)),
            pltpu.SemaphoreType.DMA((2,)),
        ],
        compiler_params=pltpu.CompilerParams(
            collective_id=0, has_side_effects=True, vmem_limit_bytes=VMEM_LIMIT
        ),
        name="gather_line",
    )(x, table, charges)


def index_kernel(w_ref, table, mine, lists, place):
    w = w_ref[0]
    before = (
        lax.broadcasted_iota(I32, (ENTRIES, ENTRIES), 0) < lax.broadcasted_iota(I32, (ENTRIES, ENTRIES), 1)
    ).astype(BF16)
    t = jnp.concatenate([table[:, j, :] for j in range(3)], axis=1)
    named = (t // 1024) == w
    rank = mm(named.astype(BF16), before).astype(I32)
    rank = jnp.where(named, rank, -1)
    ident = t % 1024
    slot = lax.broadcasted_iota(I32, (CAP, ENTRIES), 0)
    for r in range(WIDE):
        hit = jnp.where(slot == rank[r : r + 1, :], ident[r : r + 1, :], 0)
        lists[:, r : r + 1] = jnp.sum(hit, axis=1, keepdims=True)
    m = jnp.concatenate([mine[j : j + 1, :] for j in range(3)], axis=1)
    group = m // 1024
    onehot = lax.broadcasted_iota(I32, (WIDE, ENTRIES), 0) == group
    ranks = mm(onehot.astype(BF16), before).astype(I32)
    mine_rank = jnp.sum(jnp.where(onehot, ranks, 0), axis=0, keepdims=True)
    place[...] = group * CAP + mine_rank


def indices(w, table, mine):
    vm = pl.BlockSpec(memory_space=pltpu.VMEM)
    return pl.pallas_call(
        index_kernel,
        out_shape=(
            jax.ShapeDtypeStruct((CAP, WIDE), I32),
            jax.ShapeDtypeStruct((1, ENTRIES), I32),
        ),
        in_specs=[pl.BlockSpec(memory_space=pltpu.SMEM), vm, vm],
        out_specs=(vm, vm),
        name="request_lists",
    )(w, table, mine)


def pick_kernel(lists, g_ref, o_ref):
    r = pl.program_id(0)

    def step(i, c):
        for u in range(8):
            s = i * 8 + u
            o_ref[s] = g_ref[lists[s, r]]
        return c

    lax.fori_loop(0, CAP // 8, step, 0)


def pick(lists, g):
    return pl.pallas_call(
        pick_kernel,
        grid=(WIDE,),
        out_shape=jax.ShapeDtypeStruct((WIDE * CAP, 32, 128), BF16),
        in_specs=[
            pl.BlockSpec(memory_space=pltpu.SMEM),
            pl.BlockSpec(memory_space=pltpu.VMEM),
        ],
        out_specs=pl.BlockSpec((CAP, 32, 128), lambda r: (r, 0, 0)),
        compiler_params=pltpu.CompilerParams(vmem_limit_bytes=VMEM_LIMIT),
        name="pick_requested",
    )(lists, g)


ROWS = 16


def local_kernel(slots, coupling, near, x_ref, q_ref, halo, coupled, near_out, xbd, qbd, rows, nrows, v):
    g = pl.program_id(0)
    lo64 = lo_mask(64)

    @pl.when(g == 0)
    def _():
        def build(i, c):
            xbd[i] = spread(x_ref[i])
            return c

        lax.fori_loop(0, NODES, build, 0)
        eye = (
            lax.broadcasted_iota(I32, (128, 128), 0) == lax.broadcasted_iota(I32, (128, 128), 1)
        ).astype(BF16)

        def put(i, q):
            t = mm(eye, jnp.concatenate([q, q], axis=0), ((1,), (1,))).astype(BF16)
            zero = jnp.zeros((64, 128), BF16)
            for b in range(2):
                d = t[64 * b : 64 * b + 64]
                qbd[2 * i + b] = jnp.concatenate(
                    [jnp.where(lo64, d, zero), jnp.where(lo64, zero, d)], axis=0
                )

        put(0, halo[0])
        put(PARENTS + 1, halo[1])

        def build_q(i, c):
            put(i + 1, q_ref[:, pl.ds(pl.multiple_of(i * 128, 128), 128)])
            return c

        lax.fori_loop(0, PARENTS, build_q, 0)

    to_rows(coupling, rows, 32 * K_LOCAL, ROWS)

    def node(i, c):
        n = g * ROWS + i
        acc = jnp.zeros((32, 128), F32)
        a = rows[pl.ds(i, 32 * K_LOCAL, stride=ROWS), :].astype(BF16)
        offset = jnp.where(n < LEAF_DEV, 0, LEAF_DEV)
        for k in range(0, K_LOCAL, 2):
            lhs = jnp.concatenate([a[32 * k : 32 * k + 32], a[32 * k + 32 : 32 * k + 64]], axis=1)
            rhs = jnp.concatenate(
                [xbd[slots[n, k] + offset], xbd[slots[n, k + 1] + offset]], axis=0
            )
            acc = acc + mm(lhs, rhs)
        coupled[i] = acc
        return c

    lax.fori_loop(0, ROWS, node, 0)

    @pl.when(g < LEAF_DEV // ROWS)
    def _():
        to_rows(near, nrows, 160, ROWS)

        def pair(p, c):
            for b in range(2):
                i = 2 * p + b
                a = nrows[pl.ds(i, 160, stride=ROWS), :].astype(BF16)
                acc = jnp.zeros((32, 128), F32)
                for t in range(5):
                    acc = acc + mm(a[32 * t : 32 * t + 32], qbd[g * ROWS + i + t])
                unpair(v, 64 * b, acc)
            near_out[:, pl.ds(pl.multiple_of(g * (ROWS * 64) + p * 128, 128), 128)] = v[...].T[0:64]
            return c

        lax.fori_loop(0, ROWS // 2, pair, 0)


def local_part(slots, coupling, near, x, charges, halo):
    vm = pl.BlockSpec(memory_space=pltpu.VMEM)
    wl = 4096 * K_LOCAL
    return pl.pallas_call(
        local_kernel,
        grid=(NODES // ROWS,),
        out_shape=(
            jax.ShapeDtypeStruct((NODES, 32, 128), F32),
            jax.ShapeDtypeStruct((64, 4096), F32),
        ),
        in_specs=[
            pl.BlockSpec(memory_space=pltpu.SMEM),
            pl.BlockSpec((ROWS, wl), lambda g: (g, 0)),
            pl.BlockSpec((ROWS, 20480), lambda g: (jnp.minimum(g, LEAF_DEV // ROWS - 1), 0)),
            vm,
            vm,
            vm,
        ],
        out_specs=(
            pl.BlockSpec((ROWS, 32, 128), lambda g: (g, 0, 0)),
            pl.BlockSpec((64, 4096), lambda g: (0, 0)),
        ),
        scratch_shapes=[
            pltpu.VMEM((NODES, 128, 128), BF16),
            pltpu.VMEM((LEAF_DEV + 4, 128, 128), BF16),
            pltpu.VMEM((32 * K_LOCAL * ROWS, 128), F32),
            pltpu.VMEM((160 * ROWS, 128), F32),
            pltpu.VMEM((128, 128), F32),
        ],
        compiler_params=pltpu.CompilerParams(vmem_limit_bytes=VMEM_LIMIT),
        cost_estimate=pl.CostEstimate(flops=5 * 10**9, bytes_accessed=22 * 10**6, transcendentals=0),
        name="local_partners",
    )(slots, coupling, near, x, charges, halo)


def far_kernel(place, coupling, recv, local, near, transfer, basis, out, rows, trows, cp, v):
    to_rows(coupling, rows, 32 * K_FAR, NODES)
    to_rows(transfer, trows, 64, PARENTS)
    lo64 = lo_mask(64)

    def node(n, c):
        a = rows[pl.ds(n, 32 * K_FAR, stride=NODES), :].astype(BF16)
        acc = local[n]
        for k in range(0, K_FAR, 2):
            lhs = jnp.concatenate([a[32 * k : 32 * k + 32], a[32 * k + 32 : 32 * k + 64]], axis=1)
            rhs = jnp.concatenate(
                [spread(recv[place[n * K_FAR + k]]), spread(recv[place[n * K_FAR + k + 1]])], axis=0
            )
            acc = acc + mm(lhs, rhs)
        cp[n] = acc
        return c

    lax.fori_loop(0, NODES, node, 0)

    def pair(p, c):
        unpair(v, 0, cp[LEAF_DEV + p])
        d = v[0:64].astype(BF16)
        zero = jnp.zeros_like(d)
        down = jnp.concatenate([jnp.where(lo64, d, zero), jnp.where(lo64, zero, d)], axis=0)
        a = trows[pl.ds(p, 64, stride=PARENTS), :].astype(BF16)
        add = mm(a, down)
        unpair(v, 0, cp[2 * p] + add[0:32])
        unpair(v, 64, cp[2 * p + 1] + add[32:64])
        leaf_down = v[...].astype(BF16)
        cols = pl.ds(pl.multiple_of(p * 128, 128), 128)
        b = basis[:, cols]
        bb = jnp.concatenate([jnp.where(lo64, b, zero), jnp.where(lo64, zero, b)], axis=0)
        out[:, cols] = near[:, cols] + mm(leaf_down, bb, ((0,), (0,)))[0:64]
        return c

    lax.fori_loop(0, PARENTS, pair, 0)


def far_part(place, coupling, recv, local, near, transfer, basis):
    vm = pl.BlockSpec(memory_space=pltpu.VMEM)
    wf = 4096 * K_FAR
    return pl.pallas_call(
        far_kernel,
        grid=(1,),
        out_shape=jax.ShapeDtypeStruct((64, 4096), F32),
        in_specs=[
            pl.BlockSpec(memory_space=pltpu.SMEM),
            pl.BlockSpec((NODES, wf), lambda g: (0, K_LOCAL // K_FAR)),
            vm,
            vm,
            vm,
            vm,
            vm,
        ],
        out_specs=vm,
        scratch_shapes=[
            pltpu.VMEM((32 * K_FAR * NODES, 128), F32),
            pltpu.VMEM((64 * PARENTS, 128), F32),
            pltpu.VMEM((NODES, 32, 128), F32),
            pltpu.VMEM((128, 128), F32),
        ],
        compiler_params=pltpu.CompilerParams(vmem_limit_bytes=VMEM_LIMIT),
        name="far_and_down",
    )(place, coupling, recv, local, near, transfer, basis)


def shards(charges, basis, transfer, coupling, near_blocks, local_slot, owner, far_slot):
    w, n = lax.axis_index("wide"), lax.axis_index("narrow")
    me = w * NARROW + n
    offset = jnp.where(jnp.arange(NODES) < LEAF_DEV, 0, LEAF_DEV).astype(I32)[:, None]
    entry = (owner // NARROW) * 1024 + (owner % NARROW) * NODES + far_slot + offset
    mine = jnp.pad(entry.reshape(3, 128), ((0, 5), (0, 0)))
    x = coefs(charges, basis, transfer)
    g, table, halo = gather(x, mine, charges)
    keep = jnp.stack([me > 0, me < WIDE * NARROW - 1])[:, None, None]
    halo = jnp.where(keep, halo, jnp.zeros_like(halo))
    lists, place = indices(w.reshape(1).astype(I32), table, mine)
    send = pick(lists, g.reshape(NARROW * NODES, 32, 128))
    recv = lax.all_to_all(send.reshape(WIDE, CAP * 32, 128), "wide", split_axis=0, concat_axis=0, tiled=True)
    local, near = local_part(local_slot, coupling, near_blocks, x, charges, halo)
    return far_part(
        place.reshape(ENTRIES), coupling, recv.reshape(WIDE * CAP, 32, 128), local, near, transfer, basis
    )


def solution(mesh):
    cols, rows = P(None, ("wide", "narrow")), P(("wide", "narrow"), None)
    return jax.shard_map(
        shards,
        mesh=mesh,
        in_specs=(cols, cols, rows, rows, rows, rows, rows, rows),
        out_specs=cols,
        check_vma=False,
    )
```

```python
import functools

import jax
import jax.numpy as jnp
from jax import lax
from jax.experimental import pallas as pl
from jax.experimental.pallas import tpu as pltpu
from jax.sharding import PartitionSpec as P

MESH = pl.DeviceIdType.MESH
F32, BF16, I32 = jnp.float32, jnp.bfloat16, jnp.int32

WIDE, NARROW = 16, 8
LEAF_DEV, PARENTS, NODES = 64, 32, 96
K_LOCAL, K_FAR = 20, 4
DEVICES = WIDE * NARROW
TROWS = 4
UNROLL = 4
CAP = 6
HALF = CAP // 2
VMEM_LIMIT = 56 << 20


def lo_mask(rows):
    return lax.broadcasted_iota(I32, (rows, 128), 1) < 64


def swap_halves(x):
    return jnp.concatenate([x[:, 64:], x[:, :64]], axis=1)


def mm(a, b, dims=((1,), (0,))):
    return lax.dot_general(a, b, (dims, ((), ())), preferred_element_type=F32)


def spread(tile):
    lo = lo_mask(32)
    zero = jnp.zeros_like(tile)
    turned = swap_halves(tile)
    return jnp.concatenate(
        [
            jnp.where(lo, tile, zero),
            jnp.where(lo, turned, zero),
            jnp.where(lo, zero, turned),
            jnp.where(lo, zero, tile),
        ],
        axis=0,
    )


def unpair(ref, start, packed):
    lo = lo_mask(32)
    turned = swap_halves(packed)
    ref[pl.ds(start, 32, stride=2), :] = jnp.where(lo, packed, turned)
    ref[pl.ds(start + 1, 32, stride=2), :] = jnp.where(lo, turned, packed)


def to_rows(src, dst, tiles, rows):
    def step(g, c):
        for u in range(8):
            t = g * 8 + u
            dst[pl.ds(t * (rows + 1), rows), :] = src[
                :, pl.ds(pl.multiple_of(t * 128, 128), 128)
            ].astype(F32)
        return c

    lax.fori_loop(0, tiles // 8, step, 0)


def coef_kernel(charges, basis, transfer, t_ref, out, ot_ref, oh_ref, rows, v, ls, lr, ts, tr, hs, hr):
    w, n = lax.axis_index("wide"), lax.axis_index("narrow")
    me = w * NARROW + n
    nxt, prv = lax.rem(me + 1, DEVICES), lax.rem(me + DEVICES - 1, DEVICES)
    bar = pltpu.get_barrier_semaphore()
    z, x = w // 4, w % 4
    line = [lax.rem(n + d, NARROW) for d in range(1, NARROW)]
    peers = [
        lax.rem(z + dz, 4) * 4 + lax.rem(x + dx, 4)
        for dz, dx in ((2, 2), (1, 2), (2, 1), (3, 2), (2, 3), (1, 1), (3, 3), (1, 3), (3, 1), (0, 2), (2, 0), (0, 1), (1, 0), (0, 3), (3, 0))
    ]
    for p in line:
        pl.semaphore_signal(bar, inc=1, device_id=(w, p), device_id_type=MESH)
    for p in (nxt, prv):
        pl.semaphore_signal(bar, inc=1, device_id=(p // NARROW, p % NARROW), device_id_type=MESH)
    for p in peers:
        pl.semaphore_signal(bar, inc=1, device_id=(p, n), device_id_type=MESH)

    def remote(src, dst, ssem, rsem, dev):
        k = pltpu.make_async_remote_copy(
            src_ref=src, dst_ref=dst, send_sem=ssem, recv_sem=rsem, device_id=dev, device_id_type=MESH
        )
        k.start()
        return k

    to_rows(transfer, rows, 64, PARENTS)
    lo64, lo32 = lo_mask(64), lo_mask(32)

    def parent_pair(i, c):
        for u in range(UNROLL):
            p = i * UNROLL + u
            at = 128 * u
            cols = pl.ds(pl.multiple_of(p * 128, 128), 128)
            b, q = basis[:, cols], charges[:, cols]
            zero = jnp.zeros_like(b)
            bb = jnp.concatenate([jnp.where(lo64, b, zero), jnp.where(lo64, zero, b)], axis=0)
            qq = jnp.concatenate([q, q], axis=0)
            leaf = mm(bb, qq, ((1,), (1,))).astype(BF16)
            out[2 * p] = jnp.where(lo32, leaf[0:32], leaf[32:64])
            out[2 * p + 1] = jnp.where(lo32, leaf[64:96], leaf[96:128])
            v[at : at + 128] = leaf.astype(F32)
            even, odd = v[pl.ds(at, 64, stride=2), :], v[pl.ds(at + 1, 64, stride=2), :]
            paired = jnp.where(lo64, even, odd).astype(BF16)
            a = rows[pl.ds(p, 64, stride=PARENTS + 1), :].astype(BF16)
            m = mm(a, paired, ((0,), (0,)))
            s = jnp.where(lo64, m[0:64], m[64:128])
            parent = (s + swap_halves(s)).astype(BF16)
            out[LEAF_DEV + p] = jnp.where(lo32, parent[0:32], parent[32:64])
        return c

    pl.semaphore_wait(bar, 24)
    first = [remote(t_ref, ot_ref.at[w, n], ls.at[i], lr.at[i], (w, p)) for i, p in enumerate(line)]
    halos = [
        remote(charges.at[:, pl.ds(3968, 128)], oh_ref.at[0], hs.at[0], hr.at[0], (nxt // NARROW, nxt % NARROW)),
        remote(charges.at[:, pl.ds(0, 128)], oh_ref.at[1], hs.at[1], hr.at[1], (prv // NARROW, prv % NARROW)),
    ]
    ot_ref[w, n] = t_ref[...]
    quarter = PARENTS // UNROLL // 4
    lax.fori_loop(0, quarter, parent_pair, 0)
    for k in first:
        k.wait_recv()
    second = [remote(ot_ref.at[w], ot_ref.at[w], ts.at[i], tr.at[i], (p, n)) for i, p in enumerate(peers)]
    lax.fori_loop(quarter, 4 * quarter, parent_pair, 0)
    for k in second + halos:
        k.wait_recv()
    for k in first + second + halos:
        k.wait_send()


def coefs(charges, basis, transfer, table):
    vm = pl.BlockSpec(memory_space=pltpu.VMEM)
    return pl.pallas_call(
        coef_kernel,
        out_shape=(
            jax.ShapeDtypeStruct((NODES, 32, 128), BF16),
            jax.ShapeDtypeStruct((WIDE, NARROW, TROWS, 128), I32),
            jax.ShapeDtypeStruct((2, 64, 128), BF16),
        ),
        in_specs=[vm] * 4,
        out_specs=(vm, vm, vm),
        scratch_shapes=[
            pltpu.VMEM((64 * (PARENTS + 1), 128), F32),
            pltpu.VMEM((UNROLL * 128, 128), F32),
            pltpu.SemaphoreType.DMA((7,)),
            pltpu.SemaphoreType.DMA((7,)),
            pltpu.SemaphoreType.DMA((15,)),
            pltpu.SemaphoreType.DMA((15,)),
            pltpu.SemaphoreType.DMA((2,)),
            pltpu.SemaphoreType.DMA((2,)),
        ],
        compiler_params=pltpu.CompilerParams(
            collective_id=0, has_side_effects=True, vmem_limit_bytes=VMEM_LIMIT
        ),
        name="coefs_and_tables",
    )(charges, basis, transfer, table)


def index_kernel(me_ref, table, mine, lists, place):
    me = me_ref[0]
    lane = lax.broadcasted_iota(I32, (128, 128), 1)
    sub = lax.broadcasted_iota(I32, (128, 128), 0)
    for b in range(3):
        t = table[:, b, :].T
        named = (t // 128) == me
        code = sub * 128 + t % 128
        first = jnp.min(jnp.where(named, code, 128 * 128), axis=0, keepdims=True)
        last = jnp.max(jnp.where(named, code, 0), axis=0, keepdims=True)
        lists[2 * b : 2 * b + 1, :] = first % 128
        lists[2 * b + 1 : 2 * b + 2, :] = last % 128
        own = mine[b : b + 1, :] // 128
        same = jnp.broadcast_to(own, (128, 128))
        again = jnp.where((same.T == same) & (sub < lane), 1, 0)
        place[b : b + 1, :] = own * CAP + 2 * b + jnp.max(again, axis=0, keepdims=True)


def indices(me, table, mine):
    vm = pl.BlockSpec(memory_space=pltpu.VMEM)
    return pl.pallas_call(
        index_kernel,
        out_shape=(
            jax.ShapeDtypeStruct((CAP, DEVICES), I32),
            jax.ShapeDtypeStruct((3, 128), I32),
        ),
        in_specs=[pl.BlockSpec(memory_space=pltpu.SMEM), vm, vm],
        out_specs=(vm, vm),
        name="request_lists",
    )(me, table, mine)


ROWS = 16
SUBSETS = ("z", "x", "y"), ("zx", "zy", "xy"), ("zxy",)
SLOTS1, SLOTS2, SLOTS3 = 108, 36, 4


def exchange_kernel(
    lists, slots, x_ref, coupling, near, q_ref, halo, recv, coupled, near_out,
    send, relay, cbuf, nbuf, xbd, qbd, rows, nrows, v, s1, r1, s2, r2, dsem, csem, nsem,
):
    w, n = lax.axis_index("wide"), lax.axis_index("narrow")
    me = w * NARROW + n
    z, x, y, c = w // 4, w % 4, n // 2, n % 2
    wl = 4096 * K_LOCAL
    blocks = NODES // ROWS

    def load(g):
        return pltpu.make_async_copy(
            coupling.at[pl.ds(g * ROWS, ROWS), pl.ds(0, wl)], cbuf.at[g % 2], csem.at[g % 2]
        )

    load(0).start()
    near_copy = pltpu.make_async_copy(near, nbuf, nsem)
    near_copy.start()

    def device(dz, dx, dy, core):
        return (
            lax.rem(z + dz, 4) * 4 + lax.rem(x + dx, 4),
            lax.rem(y + dy, 4) * 2 + core,
        )

    bar = pltpu.get_barrier_semaphore()

    def steps(i):
        a, b, d = i // 9, (i // 3) % 3, i % 3
        return a + a // 2, b + b // 2, d + d // 2

    def greet(i, carry):
        for core in range(2):
            pl.semaphore_signal(bar, inc=1, device_id=device(*steps(i), core), device_id_type=MESH)
        return carry

    lax.fori_loop(1, 27, greet, 0)
    pl.semaphore_signal(bar, inc=1, device_id=device(0, 0, 0, 1 - c), device_id_type=MESH)

    def fill(r, carry):
        for s in range(CAP):
            send[r * CAP + s] = x_ref[jnp.minimum(lists[s, r], NODES - 1)]
        return carry

    lax.fori_loop(0, DEVICES, fill, 0)
    pl.semaphore_wait(bar, 53)

    def remote(src, dst, ssem, rsem, dev):
        return pltpu.make_async_remote_copy(
            src_ref=src, dst_ref=dst, send_sem=ssem, recv_sem=rsem, device_id=dev, device_id_type=MESH
        )

    def relayed(act):
        base = 0
        for level, subsets in enumerate(SUBSETS):
            others = (9, 3, 1)[level]

            def body(i, carry, subsets=subsets, base=base, level=level):
                for k, axes in enumerate(subsets):
                    val = [i % 3, i // 3]
                    off = {}
                    for axis in "zxy":
                        if axis in axes:
                            off[axis] = 2
                        else:
                            a = val.pop(0)
                            off[axis] = a + a // 2
                    for core in range(2):
                        for h in range(2):
                            hop = (1, 3)[h]
                            one = {axis: (hop if axis in axes else 0) for axis in "zxy"}
                            slot = base + ((i * len(subsets) + k) * 2 + core) * 2 + h
                            act(off, one, core, h, slot)
                return carry

            lax.fori_loop(0, others, body, 0)
            base += others * len(subsets) * 4

    def leg1(off, one, core, h, slot):
        tw, tn = device(off["z"], off["x"], off["y"], core)
        remote(
            send.at[pl.ds((tw * NARROW + tn) * CAP + h * HALF, HALF)],
            relay.at[pl.ds(slot * HALF, HALF)],
            s1,
            r1,
            device(one["z"], one["x"], one["y"], c),
        ).start()

    def leg2(off, one, core, h, slot):
        sw, sn = device(4 - one["z"], 4 - one["x"], 4 - one["y"], c)
        rest = {axis: off[axis] - one[axis] + 4 for axis in "zxy"}
        remote(
            relay.at[pl.ds(slot * HALF, HALF)],
            recv.at[pl.ds((sw * NARROW + sn) * CAP + h * HALF, HALF)],
            s2,
            r2,
            device(rest["z"], rest["x"], rest["y"], core),
        ).start()

    def direct(i, carry):
        j = lax.rem(i * 10, 27)
        dz, dx, dy = steps(j)
        for core in range(2):
            tw, tn = device(dz, dx, dy, core)
            remote(
                send.at[pl.ds((tw * NARROW + tn) * CAP, CAP)],
                recv.at[pl.ds(me * CAP, CAP)],
                s2,
                r2,
                (tw, tn),
            ).start()
        return carry

    relayed(leg1)
    lax.fori_loop(1, 27, direct, 0)
    tw, tn = device(0, 0, 0, 1 - c)
    remote(
        send.at[pl.ds((tw * NARROW + tn) * CAP, CAP)], recv.at[pl.ds(me * CAP, CAP)], s2, r2, (tw, tn)
    ).start()
    own = pltpu.make_async_copy(send.at[pl.ds(me * CAP, CAP)], recv.at[pl.ds(me * CAP, CAP)], dsem)
    own.start()

    lo64 = lo_mask(64)

    def build(i, carry):
        xbd[i] = spread(x_ref[i])
        return carry

    lax.fori_loop(0, NODES, build, 0)

    def compute(g):
        if g + 1 < blocks:
            load(g + 1).start()
        load(g).wait()
        to_rows(cbuf.at[g % 2], rows, 32 * K_LOCAL, ROWS)
        offset = 0 if g * ROWS < LEAF_DEV else LEAF_DEV

        def node(i, carry):
            acc = jnp.zeros((32, 128), F32)
            a = rows[pl.ds(i, 32 * K_LOCAL, stride=ROWS + 1), :].astype(BF16)
            for k in range(0, K_LOCAL, 2):
                lhs = jnp.concatenate([a[32 * k : 32 * k + 32], a[32 * k + 32 : 32 * k + 64]], axis=1)
                row = g * ROWS + i
                rhs = jnp.concatenate(
                    [xbd[slots[k, row] + offset], xbd[slots[k + 1, row] + offset]], axis=0
                )
                acc = acc + mm(lhs, rhs)
            coupled[g * ROWS + i] = acc
            return carry

        lax.fori_loop(0, ROWS, node, 0, unroll=2)

    def build_near():
        eye = (
            lax.broadcasted_iota(I32, (128, 128), 0) == lax.broadcasted_iota(I32, (128, 128), 1)
        ).astype(BF16)

        def put(i, q):
            t = mm(eye, jnp.concatenate([q, q], axis=0), ((1,), (1,))).astype(BF16)
            zero = jnp.zeros((64, 128), BF16)
            for b in range(2):
                d = t[64 * b : 64 * b + 64]
                qbd[2 * i + b] = jnp.concatenate(
                    [jnp.where(lo64, d, zero), jnp.where(lo64, zero, d)], axis=0
                )

        put(0, halo[0])
        put(PARENTS + 1, halo[1])

        def build_q(i, carry):
            put(i + 1, q_ref[:, pl.ds(pl.multiple_of(i * 128, 128), 128)])
            return carry

        lax.fori_loop(0, PARENTS, build_q, 0)
        near_copy.wait()

    def compute_near(g):
        to_rows(nbuf.at[pl.ds(g * ROWS, ROWS)], nrows, 160, ROWS)

        def pair(i, carry):
            for u in range(2):
                p = 2 * i + u
                for b in range(2):
                    a = nrows[pl.ds(2 * p + b, 160, stride=ROWS + 1), :].astype(BF16)
                    acc = jnp.zeros((32, 128), F32)
                    for t in range(5):
                        acc = acc + mm(a[32 * t : 32 * t + 32], qbd[g * ROWS + 2 * p + b + t])
                    unpair(v, 128 * u + 64 * b, acc)
                near_out[:, pl.ds(pl.multiple_of(g * (ROWS * 64) + p * 128, 128), 128)] = v[
                    128 * u : 128 * u + 128
                ].T[0:64]
            return carry

        lax.fori_loop(0, ROWS // 4, pair, 0)

    compute(0)
    compute(1)
    compute(2)
    build_near()
    total = 148 * HALF
    pltpu.make_async_copy(relay, relay, r1).wait()
    relayed(leg2)
    compute(3)
    compute(4)
    compute(5)
    for g in range(LEAF_DEV // ROWS):
        compute_near(g)
    own.wait()
    part = recv.at[pl.ds(0, 127 * CAP)]
    pltpu.make_async_copy(part, part, r2).wait()
    pltpu.make_async_copy(relay, relay, s1).wait()
    pltpu.make_async_copy(part, part, s2).wait()


def exchange(lists, slots, x, coupling, near, charges, halo):
    vm = pl.BlockSpec(memory_space=pltpu.VMEM)
    sm = pl.BlockSpec(memory_space=pltpu.SMEM)
    hbm = pl.BlockSpec(memory_space=pl.ANY)
    return pl.pallas_call(
        exchange_kernel,
        out_shape=(
            jax.ShapeDtypeStruct((DEVICES * CAP, 32, 128), BF16),
            jax.ShapeDtypeStruct((NODES, 32, 128), F32),
            jax.ShapeDtypeStruct((64, 4096), F32),
        ),
        in_specs=[sm, sm, vm, hbm, hbm, vm, vm],
        out_specs=(vm, vm, vm),
        scratch_shapes=[
            pltpu.VMEM((DEVICES * CAP, 32, 128), BF16),
            pltpu.VMEM((148 * HALF, 32, 128), BF16),
            pltpu.VMEM((2, ROWS, 4096 * K_LOCAL), BF16),
            pltpu.VMEM((LEAF_DEV, 20480), BF16),
            pltpu.VMEM((NODES, 128, 128), BF16),
            pltpu.VMEM((LEAF_DEV + 4, 128, 128), BF16),
            pltpu.VMEM((32 * K_LOCAL * (ROWS + 1), 128), F32),
            pltpu.VMEM((160 * (ROWS + 1), 128), F32),
            pltpu.VMEM((256, 128), F32),
            pltpu.SemaphoreType.DMA,
            pltpu.SemaphoreType.DMA,
            pltpu.SemaphoreType.DMA,
            pltpu.SemaphoreType.DMA,
            pltpu.SemaphoreType.DMA,
            pltpu.SemaphoreType.DMA((2,)),
            pltpu.SemaphoreType.DMA,
        ],
        compiler_params=pltpu.CompilerParams(
            collective_id=1, has_side_effects=True, vmem_limit_bytes=VMEM_LIMIT
        ),
        name="exchange_beside_local",
    )(lists, slots, x, coupling, near, charges, halo)


def far_kernel(place, coupling, recv, local, near, transfer, basis, out, rows, trows, cp, v):
    to_rows(coupling, rows, 32 * K_FAR, NODES)
    to_rows(transfer, trows, 64, PARENTS)
    lo64 = lo_mask(64)

    def node(n, c):
        a = rows[pl.ds(n, 32 * K_FAR, stride=NODES + 1), :].astype(BF16)
        acc = local[n]
        for k in range(0, K_FAR, 2):
            lhs = jnp.concatenate([a[32 * k : 32 * k + 32], a[32 * k + 32 : 32 * k + 64]], axis=1)
            rhs = jnp.concatenate(
                [spread(recv[place[n // 32, (n % 32) * K_FAR + k]]), spread(recv[place[n // 32, (n % 32) * K_FAR + k + 1]])], axis=0
            )
            acc = acc + mm(lhs, rhs)
        cp[n] = acc
        return c

    lax.fori_loop(0, NODES, node, 0, unroll=4)

    def pair(i, c):
        for u in range(UNROLL):
            p = i * UNROLL + u
            at = 128 * u
            unpair(v, at, cp[LEAF_DEV + p])
            d = v[at : at + 64].astype(BF16)
            zero = jnp.zeros_like(d)
            down = jnp.concatenate([jnp.where(lo64, d, zero), jnp.where(lo64, zero, d)], axis=0)
            a = trows[pl.ds(p, 64, stride=PARENTS + 1), :].astype(BF16)
            add = mm(a, down)
            unpair(v, at, cp[2 * p] + add[0:32])
            unpair(v, at + 64, cp[2 * p + 1] + add[32:64])
            leaf_down = v[at : at + 128].astype(BF16)
            cols = pl.ds(pl.multiple_of(p * 128, 128), 128)
            b = basis[:, cols]
            bb = jnp.concatenate([jnp.where(lo64, b, zero), jnp.where(lo64, zero, b)], axis=0)
            out[:, cols] = near[:, cols] + mm(leaf_down, bb, ((0,), (0,)))[0:64]
        return c

    lax.fori_loop(0, PARENTS // UNROLL, pair, 0)


def far_part(place, coupling, recv, local, near, transfer, basis):
    vm = pl.BlockSpec(memory_space=pltpu.VMEM)
    wf = 4096 * K_FAR
    return pl.pallas_call(
        far_kernel,
        grid=(1,),
        out_shape=jax.ShapeDtypeStruct((64, 4096), F32),
        in_specs=[
            pl.BlockSpec(memory_space=pltpu.SMEM),
            pl.BlockSpec((NODES, wf), lambda g: (0, K_LOCAL // K_FAR)),
            vm,
            vm,
            vm,
            vm,
            vm,
        ],
        out_specs=vm,
        scratch_shapes=[
            pltpu.VMEM((32 * K_FAR * (NODES + 1), 128), F32),
            pltpu.VMEM((64 * (PARENTS + 1), 128), F32),
            pltpu.VMEM((NODES, 32, 128), F32),
            pltpu.VMEM((UNROLL * 128, 128), F32),
        ],
        compiler_params=pltpu.CompilerParams(vmem_limit_bytes=VMEM_LIMIT),
        name="far_and_down",
    )(place, coupling, recv, local, near, transfer, basis)


def shards(charges, basis, transfer, coupling, near_blocks, local_slot, owner, far_slot):
    w, n = lax.axis_index("wide"), lax.axis_index("narrow")
    me = w * NARROW + n
    offset = jnp.where(jnp.arange(NODES) < LEAF_DEV, 0, LEAF_DEV).astype(I32)[:, None]
    entry = (owner * 128 + far_slot + offset).reshape(3, 128)
    mine = jnp.pad(entry, ((0, TROWS - 3), (0, 0)))
    x, table, halo = coefs(charges, basis, transfer, mine)
    keep = jnp.stack([me > 0, me < DEVICES - 1])[:, None, None]
    halo = jnp.where(keep, halo, jnp.zeros_like(halo))
    lists, place = indices(me.reshape(1).astype(I32), table.reshape(DEVICES, TROWS, 128), mine)
    recv, local, near = exchange(lists, local_slot.T, x, coupling, near_blocks, charges, halo)
    return far_part(place, coupling, recv, local, near, transfer, basis)


def solution(mesh):
    cols, rows = P(None, ("wide", "narrow")), P(("wide", "narrow"), None)
    return jax.shard_map(
        shards,
        mesh=mesh,
        in_specs=(cols, cols, rows, rows, rows, rows, rows, rows),
        out_specs=cols,
        check_vma=False,
    )
```

```python
import functools

import jax
import jax.numpy as jnp
from jax import lax
from jax.experimental import pallas as pl
from jax.experimental.pallas import tpu as pltpu
from jax.sharding import PartitionSpec as P

MESH = pl.DeviceIdType.MESH
F32, BF16, I32 = jnp.float32, jnp.bfloat16, jnp.int32

WIDE, NARROW = 16, 8
LEAF_DEV, PARENTS, NODES = 64, 32, 96
K_LOCAL, K_FAR = 20, 4
DEVICES = WIDE * NARROW
TROWS = 4
UNROLL = 4
CAP = 6
HALF = CAP // 2
VMEM_LIMIT = 56 << 20


def lo_mask(rows):
    return lax.broadcasted_iota(I32, (rows, 128), 1) < 64


def swap_halves(x):
    return jnp.concatenate([x[:, 64:], x[:, :64]], axis=1)


def mm(a, b, dims=((1,), (0,))):
    return lax.dot_general(a, b, (dims, ((), ())), preferred_element_type=F32)


def spread(tile):
    lo = lo_mask(32)
    zero = jnp.zeros_like(tile)
    turned = swap_halves(tile)
    return jnp.concatenate(
        [
            jnp.where(lo, tile, zero),
            jnp.where(lo, turned, zero),
            jnp.where(lo, zero, turned),
            jnp.where(lo, zero, tile),
        ],
        axis=0,
    )


def unpair(ref, start, packed):
    lo = lo_mask(32)
    turned = swap_halves(packed)
    ref[pl.ds(start, 32, stride=2), :] = jnp.where(lo, packed, turned)
    ref[pl.ds(start + 1, 32, stride=2), :] = jnp.where(lo, turned, packed)


def to_rows(src, dst, tiles, rows):
    def step(g, c):
        for u in range(8):
            t = g * 8 + u
            dst[pl.ds(t * (rows + 1), rows), :] = src[
                :, pl.ds(pl.multiple_of(t * 128, 128), 128)
            ].astype(F32)
        return c

    lax.fori_loop(0, tiles // 8, step, 0)


def coef_kernel(charges, basis, transfer, t_ref, out, ot_ref, oh_ref, rows, v, ls, lr, ts, tr, hs, hr):
    w, n = lax.axis_index("wide"), lax.axis_index("narrow")
    me = w * NARROW + n
    nxt, prv = lax.rem(me + 1, DEVICES), lax.rem(me + DEVICES - 1, DEVICES)
    bar = pltpu.get_barrier_semaphore()
    z, x = w // 4, w % 4
    line = [lax.rem(n + d, NARROW) for d in range(1, NARROW)]
    peers = [
        lax.rem(z + dz, 4) * 4 + lax.rem(x + dx, 4)
        for dz, dx in ((2, 2), (1, 2), (2, 1), (3, 2), (2, 3), (1, 1), (3, 3), (1, 3), (3, 1), (0, 2), (2, 0), (0, 1), (1, 0), (0, 3), (3, 0))
    ]
    for p in line:
        pl.semaphore_signal(bar, inc=1, device_id=(w, p), device_id_type=MESH)
    for p in (nxt, prv):
        pl.semaphore_signal(bar, inc=1, device_id=(p // NARROW, p % NARROW), device_id_type=MESH)
    for p in peers:
        pl.semaphore_signal(bar, inc=1, device_id=(p, n), device_id_type=MESH)

    def remote(src, dst, ssem, rsem, dev):
        k = pltpu.make_async_remote_copy(
            src_ref=src, dst_ref=dst, send_sem=ssem, recv_sem=rsem, device_id=dev, device_id_type=MESH
        )
        k.start()
        return k

    to_rows(transfer, rows, 64, PARENTS)
    lo64, lo32 = lo_mask(64), lo_mask(32)

    def parent_pair(i, c):
        for u in range(UNROLL):
            p = i * UNROLL + u
            at = 128 * u
            cols = pl.ds(pl.multiple_of(p * 128, 128), 128)
            b, q = basis[:, cols], charges[:, cols]
            zero = jnp.zeros_like(b)
            bb = jnp.concatenate([jnp.where(lo64, b, zero), jnp.where(lo64, zero, b)], axis=0)
            qq = jnp.concatenate([q, q], axis=0)
            leaf = mm(bb, qq, ((1,), (1,))).astype(BF16)
            out[2 * p] = jnp.where(lo32, leaf[0:32], leaf[32:64])
            out[2 * p + 1] = jnp.where(lo32, leaf[64:96], leaf[96:128])
            v[at : at + 128] = leaf.astype(F32)
            even, odd = v[pl.ds(at, 64, stride=2), :], v[pl.ds(at + 1, 64, stride=2), :]
            paired = jnp.where(lo64, even, odd).astype(BF16)
            a = rows[pl.ds(p, 64, stride=PARENTS + 1), :].astype(BF16)
            m = mm(a, paired, ((0,), (0,)))
            s = jnp.where(lo64, m[0:64], m[64:128])
            parent = (s + swap_halves(s)).astype(BF16)
            out[LEAF_DEV + p] = jnp.where(lo32, parent[0:32], parent[32:64])
        return c

    pl.semaphore_wait(bar, 24)
    first = [remote(t_ref, ot_ref.at[w, n], ls.at[i], lr.at[i], (w, p)) for i, p in enumerate(line)]
    halos = [
        remote(charges.at[:, pl.ds(3968, 128)], oh_ref.at[0], hs.at[0], hr.at[0], (nxt // NARROW, nxt % NARROW)),
        remote(charges.at[:, pl.ds(0, 128)], oh_ref.at[1], hs.at[1], hr.at[1], (prv // NARROW, prv % NARROW)),
    ]
    ot_ref[w, n] = t_ref[...]
    quarter = PARENTS // UNROLL // 4
    lax.fori_loop(0, quarter, parent_pair, 0)
    for k in first:
        k.wait_recv()
    second = [remote(ot_ref.at[w], ot_ref.at[w], ts.at[i], tr.at[i], (p, n)) for i, p in enumerate(peers)]
    lax.fori_loop(quarter, 4 * quarter, parent_pair, 0)
    for k in second + halos:
        k.wait_recv()
    for k in first + second + halos:
        k.wait_send()


def coefs(charges, basis, transfer, table):
    vm = pl.BlockSpec(memory_space=pltpu.VMEM)
    return pl.pallas_call(
        coef_kernel,
        out_shape=(
            jax.ShapeDtypeStruct((NODES, 32, 128), BF16),
            jax.ShapeDtypeStruct((WIDE, NARROW, TROWS, 128), I32),
            jax.ShapeDtypeStruct((2, 64, 128), BF16),
        ),
        in_specs=[vm] * 4,
        out_specs=(vm, vm, vm),
        scratch_shapes=[
            pltpu.VMEM((64 * (PARENTS + 1), 128), F32),
            pltpu.VMEM((UNROLL * 128, 128), F32),
            pltpu.SemaphoreType.DMA((7,)),
            pltpu.SemaphoreType.DMA((7,)),
            pltpu.SemaphoreType.DMA((15,)),
            pltpu.SemaphoreType.DMA((15,)),
            pltpu.SemaphoreType.DMA((2,)),
            pltpu.SemaphoreType.DMA((2,)),
        ],
        compiler_params=pltpu.CompilerParams(
            collective_id=0, has_side_effects=True, vmem_limit_bytes=VMEM_LIMIT
        ),
        name="coefs_and_tables",
    )(charges, basis, transfer, table)


def index_kernel(me_ref, table, mine, lists, place):
    me = me_ref[0]
    lane = lax.broadcasted_iota(I32, (128, 128), 1)
    sub = lax.broadcasted_iota(I32, (128, 128), 0)
    for b in range(3):
        t = table[:, b, :].T
        named = (t // 128) == me
        code = sub * 128 + t % 128
        first = jnp.min(jnp.where(named, code, 128 * 128), axis=0, keepdims=True)
        last = jnp.max(jnp.where(named, code, 0), axis=0, keepdims=True)
        lists[2 * b : 2 * b + 1, :] = first % 128
        lists[2 * b + 1 : 2 * b + 2, :] = last % 128
        own = mine[b : b + 1, :] // 128
        same = jnp.broadcast_to(own, (128, 128))
        again = jnp.where((same.T == same) & (sub < lane), 1, 0)
        place[b : b + 1, :] = own * CAP + 2 * b + jnp.max(again, axis=0, keepdims=True)


def indices(me, table, mine):
    vm = pl.BlockSpec(memory_space=pltpu.VMEM)
    return pl.pallas_call(
        index_kernel,
        out_shape=(
            jax.ShapeDtypeStruct((CAP, DEVICES), I32),
            jax.ShapeDtypeStruct((3, 128), I32),
        ),
        in_specs=[pl.BlockSpec(memory_space=pltpu.SMEM), vm, vm],
        out_specs=(vm, vm),
        name="request_lists",
    )(me, table, mine)


ROWS = 16
SUBSETS = ("z", "x", "y"), ("zx", "zy", "xy"), ("zxy",)
SLOTS1, SLOTS2, SLOTS3 = 108, 36, 4


def exchange_kernel(
    lists, slots, place, x_ref, coupling, near, q_ref, halo, transfer, basis, out,
    recv, coupled, send, relay, cbuf, nbuf, xbd, qbd, rows, nrows, trows, far_lhs, down_lhs, bbd,
    v, s1, r1, s2, r2, dsem, csem, nsem,
):
    w, n = lax.axis_index("wide"), lax.axis_index("narrow")
    me = w * NARROW + n
    z, x, y, c = w // 4, w % 4, n // 2, n % 2
    tiles = 32 * (K_LOCAL + K_FAR)
    blocks = NODES // ROWS

    def load(g):
        return pltpu.make_async_copy(
            coupling.at[pl.ds(g * ROWS, ROWS)], cbuf.at[g % 2], csem.at[g % 2]
        )

    load(0).start()
    near_copy = pltpu.make_async_copy(near, nbuf, nsem)
    near_copy.start()

    def device(dz, dx, dy, core):
        return (
            lax.rem(z + dz, 4) * 4 + lax.rem(x + dx, 4),
            lax.rem(y + dy, 4) * 2 + core,
        )

    bar = pltpu.get_barrier_semaphore()

    def steps(i):
        a, b, d = i // 9, (i // 3) % 3, i % 3
        return a + a // 2, b + b // 2, d + d // 2

    def greet(i, carry):
        for core in range(2):
            pl.semaphore_signal(bar, inc=1, device_id=device(*steps(i), core), device_id_type=MESH)
        return carry

    lax.fori_loop(1, 27, greet, 0)
    pl.semaphore_signal(bar, inc=1, device_id=device(0, 0, 0, 1 - c), device_id_type=MESH)

    def fill(r, carry):
        for s in range(CAP):
            send[r * CAP + s] = x_ref[jnp.minimum(lists[s, r], NODES - 1)]
        return carry

    lax.fori_loop(0, DEVICES, fill, 0)
    pl.semaphore_wait(bar, 53)

    def remote(src, dst, ssem, rsem, dev):
        return pltpu.make_async_remote_copy(
            src_ref=src, dst_ref=dst, send_sem=ssem, recv_sem=rsem, device_id=dev, device_id_type=MESH
        )

    def relayed(act):
        base = 0
        for level, subsets in enumerate(SUBSETS):
            others = (9, 3, 1)[level]

            def body(i, carry, subsets=subsets, base=base, level=level):
                for core in range(2):
                    for h in range(2):
                        for k, axes in enumerate(subsets):
                            val = [i % 3, i // 3]
                            off = {}
                            for axis in "zxy":
                                if axis in axes:
                                    off[axis] = 2
                                else:
                                    a = val.pop(0)
                                    off[axis] = a + a // 2
                            hop = (1, 3)[h]
                            one = {axis: (hop if axis in axes else 0) for axis in "zxy"}
                            slot = base + ((i * len(subsets) + k) * 2 + core) * 2 + h
                            act(off, one, core, h, slot)
                return carry

            lax.fori_loop(0, others, body, 0)
            base += others * len(subsets) * 4

    def leg1(off, one, core, h, slot):
        tw, tn = device(off["z"], off["x"], off["y"], core)
        remote(
            send.at[pl.ds((tw * NARROW + tn) * CAP + h * HALF, HALF)],
            relay.at[pl.ds(slot * HALF, HALF)],
            s1,
            r1,
            device(one["z"], one["x"], one["y"], c),
        ).start()

    def leg2(off, one, core, h, slot):
        sw, sn = device(4 - one["z"], 4 - one["x"], 4 - one["y"], c)
        rest = {axis: off[axis] - one[axis] + 4 for axis in "zxy"}
        remote(
            relay.at[pl.ds(slot * HALF, HALF)],
            recv.at[pl.ds((sw * NARROW + sn) * CAP + h * HALF, HALF)],
            s2,
            r2,
            device(rest["z"], rest["x"], rest["y"], core),
        ).start()

    def direct(i, carry):
        j = lax.rem(i * 10, 27)
        dz, dx, dy = steps(j)
        for core in range(2):
            tw, tn = device(dz, dx, dy, core)
            remote(
                send.at[pl.ds((tw * NARROW + tn) * CAP, CAP)],
                recv.at[pl.ds(me * CAP, CAP)],
                s2,
                r2,
                (tw, tn),
            ).start()
        return carry

    relayed(leg1)
    lax.fori_loop(1, 27, direct, 0)
    tw, tn = device(0, 0, 0, 1 - c)
    remote(
        send.at[pl.ds((tw * NARROW + tn) * CAP, CAP)], recv.at[pl.ds(me * CAP, CAP)], s2, r2, (tw, tn)
    ).start()
    own = pltpu.make_async_copy(send.at[pl.ds(me * CAP, CAP)], recv.at[pl.ds(me * CAP, CAP)], dsem)
    own.start()

    lo64 = lo_mask(64)

    def build(i, carry):
        xbd[i] = spread(x_ref[i])
        return carry

    lax.fori_loop(0, NODES, build, 0)

    def compute(g):
        if g + 1 < blocks:
            load(g + 1).start()
        load(g).wait()
        to_rows(cbuf.at[g % 2], rows, tiles, ROWS)
        offset = 0 if g * ROWS < LEAF_DEV else LEAF_DEV

        def node(i, carry):
            acc = jnp.zeros((32, 128), F32)
            row = g * ROWS + i
            a = rows[pl.ds(i, tiles, stride=ROWS + 1), :].astype(BF16)
            for k in range(K_FAR):
                at = 32 * (K_LOCAL + k)
                far_lhs[row, :, 128 * k : 128 * k + 128] = a[at : at + 32]
            for k in range(0, K_LOCAL, 2):
                lhs = jnp.concatenate([a[32 * k : 32 * k + 32], a[32 * k + 32 : 32 * k + 64]], axis=1)
                rhs = jnp.concatenate(
                    [xbd[slots[k, row] + offset], xbd[slots[k + 1, row] + offset]], axis=0
                )
                acc = acc + mm(lhs, rhs)
            coupled[row] = acc
            return carry

        lax.fori_loop(0, ROWS, node, 0, unroll=2)

    def build_near():
        eye = (
            lax.broadcasted_iota(I32, (128, 128), 0) == lax.broadcasted_iota(I32, (128, 128), 1)
        ).astype(BF16)

        def put(i, q):
            t = mm(eye, jnp.concatenate([q, q], axis=0), ((1,), (1,))).astype(BF16)
            zero = jnp.zeros((64, 128), BF16)
            for b in range(2):
                d = t[64 * b : 64 * b + 64]
                qbd[2 * i + b] = jnp.concatenate(
                    [jnp.where(lo64, d, zero), jnp.where(lo64, zero, d)], axis=0
                )

        put(0, halo[0])
        put(PARENTS + 1, halo[1])

        def build_q(i, carry):
            put(i + 1, q_ref[:, pl.ds(pl.multiple_of(i * 128, 128), 128)])
            return carry

        lax.fori_loop(0, PARENTS, build_q, 0)
        near_copy.wait()

    def compute_near(g):
        to_rows(nbuf.at[pl.ds(g * ROWS, ROWS)], nrows, 160, ROWS)

        def pair(i, carry):
            for u in range(2):
                p = 2 * i + u
                for b in range(2):
                    a = nrows[pl.ds(2 * p + b, 160, stride=ROWS + 1), :].astype(BF16)
                    acc = jnp.zeros((32, 128), F32)
                    for t in range(5):
                        acc = acc + mm(a[32 * t : 32 * t + 32], qbd[g * ROWS + 2 * p + b + t])
                    unpair(v, 128 * u + 64 * b, acc)
                out[:, pl.ds(pl.multiple_of(g * (ROWS * 64) + p * 128, 128), 128)] = v[
                    128 * u : 128 * u + 128
                ].T[0:64]
            return carry

        lax.fori_loop(0, ROWS // 4, pair, 0)

    def build_down():
        to_rows(transfer, trows, 64, PARENTS)
        zero = jnp.zeros((64, 128), BF16)

        def step(i, carry):
            for u in range(UNROLL):
                p = i * UNROLL + u
                down_lhs[p] = trows[pl.ds(p, 64, stride=PARENTS + 1), :].astype(BF16)
                b = basis[:, pl.ds(pl.multiple_of(p * 128, 128), 128)]
                bbd[p] = jnp.concatenate([jnp.where(lo64, b, zero), jnp.where(lo64, zero, b)], axis=0)
            return carry

        lax.fori_loop(0, PARENTS // UNROLL, step, 0)

    def far_node(n, carry):
        acc = coupled[n]
        for k in range(0, K_FAR, 2):
            first = recv[place[n // 32, (n % 32) * K_FAR + k]]
            second = recv[place[n // 32, (n % 32) * K_FAR + k + 1]]
            rhs = jnp.concatenate([spread(first), spread(second)], axis=0)
            acc = acc + mm(far_lhs[n, :, 128 * k : 128 * k + 256], rhs)
        coupled[n] = acc
        return carry

    def way_down(i, carry):
        for u in range(UNROLL):
            p = i * UNROLL + u
            at = 128 * u
            unpair(v, at, coupled[LEAF_DEV + p])
            d = v[at : at + 64].astype(BF16)
            zero = jnp.zeros_like(d)
            down = jnp.concatenate([jnp.where(lo64, d, zero), jnp.where(lo64, zero, d)], axis=0)
            add = mm(down_lhs[p], down)
            unpair(v, at, coupled[2 * p] + add[0:32])
            unpair(v, at + 64, coupled[2 * p + 1] + add[32:64])
            leaf_down = v[at : at + 128].astype(BF16)
            cols = pl.ds(pl.multiple_of(p * 128, 128), 128)
            out[:, cols] = out[:, cols] + mm(leaf_down, bbd[p], ((0,), (0,)))[0:64]
        return carry

    compute(0)
    compute(1)
    compute(2)
    build_near()
    pltpu.make_async_copy(relay, relay, r1).wait()
    relayed(leg2)
    compute(3)
    compute(4)
    compute(5)
    for g in range(LEAF_DEV // ROWS):
        compute_near(g)
    build_down()
    own.wait()
    part = recv.at[pl.ds(0, 127 * CAP)]
    pltpu.make_async_copy(part, part, r2).wait()
    lax.fori_loop(0, NODES, far_node, 0, unroll=4)
    lax.fori_loop(0, PARENTS // UNROLL, way_down, 0)
    pltpu.make_async_copy(relay, relay, s1).wait()
    pltpu.make_async_copy(part, part, s2).wait()


def exchange(lists, slots, place, x, coupling, near, charges, halo, transfer, basis):
    vm = pl.BlockSpec(memory_space=pltpu.VMEM)
    sm = pl.BlockSpec(memory_space=pltpu.SMEM)
    hbm = pl.BlockSpec(memory_space=pl.ANY)
    return pl.pallas_call(
        exchange_kernel,
        out_shape=jax.ShapeDtypeStruct((64, 4096), F32),
        in_specs=[sm, sm, sm, vm, hbm, hbm, vm, vm, vm, vm],
        out_specs=vm,
        scratch_shapes=[
            pltpu.VMEM((DEVICES * CAP, 32, 128), BF16),
            pltpu.VMEM((NODES, 32, 128), F32),
            pltpu.VMEM((DEVICES * CAP, 32, 128), BF16),
            pltpu.VMEM((148 * HALF, 32, 128), BF16),
            pltpu.VMEM((2, ROWS, 4096 * (K_LOCAL + K_FAR)), BF16),
            pltpu.VMEM((LEAF_DEV, 20480), BF16),
            pltpu.VMEM((NODES, 128, 128), BF16),
            pltpu.VMEM((LEAF_DEV + 4, 128, 128), BF16),
            pltpu.VMEM((32 * (K_LOCAL + K_FAR) * (ROWS + 1), 128), F32),
            pltpu.VMEM((160 * (ROWS + 1), 128), F32),
            pltpu.VMEM((64 * (PARENTS + 1), 128), F32),
            pltpu.VMEM((NODES, 32, 128 * K_FAR), BF16),
            pltpu.VMEM((PARENTS, 64, 128), BF16),
            pltpu.VMEM((PARENTS, 128, 128), BF16),
            pltpu.VMEM((UNROLL * 128, 128), F32),
            pltpu.SemaphoreType.DMA,
            pltpu.SemaphoreType.DMA,
            pltpu.SemaphoreType.DMA,
            pltpu.SemaphoreType.DMA,
            pltpu.SemaphoreType.DMA,
            pltpu.SemaphoreType.DMA((2,)),
            pltpu.SemaphoreType.DMA,
        ],
        compiler_params=pltpu.CompilerParams(
            collective_id=1, has_side_effects=True, vmem_limit_bytes=VMEM_LIMIT
        ),
        name="exchange_and_products",
    )(lists, slots, place, x, coupling, near, charges, halo, transfer, basis)


def shards(charges, basis, transfer, coupling, near_blocks, local_slot, owner, far_slot):
    w, n = lax.axis_index("wide"), lax.axis_index("narrow")
    me = w * NARROW + n
    offset = jnp.where(jnp.arange(NODES) < LEAF_DEV, 0, LEAF_DEV).astype(I32)[:, None]
    entry = (owner * 128 + far_slot + offset).reshape(3, 128)
    mine = jnp.pad(entry, ((0, TROWS - 3), (0, 0)))
    x, table, halo = coefs(charges, basis, transfer, mine)
    keep = jnp.stack([me > 0, me < DEVICES - 1])[:, None, None]
    halo = jnp.where(keep, halo, jnp.zeros_like(halo))
    lists, place = indices(me.reshape(1).astype(I32), table.reshape(DEVICES, TROWS, 128), mine)
    return exchange(lists, local_slot.T, place, x, coupling, near_blocks, charges, halo, transfer, basis)


def solution(mesh):
    cols, rows = P(None, ("wide", "narrow")), P(("wide", "narrow"), None)
    return jax.shard_map(
        shards,
        mesh=mesh,
        in_specs=(cols, cols, rows, rows, rows, rows, rows, rows),
        out_specs=cols,
        check_vma=False,
    )
```

```python
import functools

import jax
import jax.numpy as jnp
from jax import lax
from jax.experimental import pallas as pl
from jax.experimental.pallas import tpu as pltpu
from jax.sharding import PartitionSpec as P

MESH = pl.DeviceIdType.MESH
F32, BF16, I32 = jnp.float32, jnp.bfloat16, jnp.int32

WIDE, NARROW = 16, 8
LEAF_DEV, PARENTS, NODES = 64, 32, 96
K_LOCAL, K_FAR = 20, 4
DEVICES = WIDE * NARROW
BLOCKS = 3
TROWS = 4
UNROLL = 4
CAP = 6
HALF = CAP // 2
VMEM_LIMIT = 56 << 20


def lo_mask(rows):
    return lax.broadcasted_iota(I32, (rows, 128), 1) < 64


def swap_halves(x):
    return jnp.concatenate([x[:, 64:], x[:, :64]], axis=1)


def mm(a, b, dims=((1,), (0,))):
    return lax.dot_general(a, b, (dims, ((), ())), preferred_element_type=F32)


def spread(tile):
    lo = lo_mask(32)
    zero = jnp.zeros_like(tile)
    turned = swap_halves(tile)
    return jnp.concatenate(
        [
            jnp.where(lo, tile, zero),
            jnp.where(lo, turned, zero),
            jnp.where(lo, zero, turned),
            jnp.where(lo, zero, tile),
        ],
        axis=0,
    )


def unpair(ref, start, packed):
    lo = lo_mask(32)
    turned = swap_halves(packed)
    ref[pl.ds(start, 32, stride=2), :] = jnp.where(lo, packed, turned)
    ref[pl.ds(start + 1, 32, stride=2), :] = jnp.where(lo, turned, packed)


def to_rows(src, dst, tiles, rows):
    def step(g, c):
        for u in range(8):
            t = g * 8 + u
            dst[pl.ds(t * (rows + 1), rows), :] = src[
                :, pl.ds(pl.multiple_of(t * 128, 128), 128)
            ].astype(F32)
        return c

    lax.fori_loop(0, tiles // 8, step, 0)


ROWS = 16
SUBSETS = ("z", "x", "y"), ("zx", "zy", "xy"), ("zxy",)
SLOTS1, SLOTS2, SLOTS3 = 108, 36, 4


def product_kernel(
    slots, mine, coupling, near, q_ref, transfer, basis, out,
    x_ref, table, halo, listv, placev, lists, place, recv, coupled, send, relay, cbuf, nbuf, xbd, qbd, rows, nrows, trows, far_lhs, down_lhs, bbd,
    v, s1, r1, s2, r2, dsem, csem, nsem, ls, lr, ts, tr, hs, hr, ps,
):
    w, n = lax.axis_index("wide"), lax.axis_index("narrow")
    me = w * NARROW + n
    z, x, y, c = w // 4, w % 4, n // 2, n % 2
    tiles = 32 * (K_LOCAL + K_FAR)
    blocks = NODES // ROWS

    def load(g):
        return pltpu.make_async_copy(
            coupling.at[pl.ds(g * ROWS, ROWS)], cbuf.at[g % 2], csem.at[g % 2]
        )

    load(0).start()
    near_copy = pltpu.make_async_copy(near, nbuf, nsem)
    near_copy.start()

    def device(dz, dx, dy, core):
        return (
            lax.rem(z + dz, 4) * 4 + lax.rem(x + dx, 4),
            lax.rem(y + dy, 4) * 2 + core,
        )

    bar = pltpu.get_barrier_semaphore()

    def steps(i):
        a, b, d = i // 9, (i // 3) % 3, i % 3
        return a + a // 2, b + b // 2, d + d // 2

    def greet(i, carry):
        for core in range(2):
            pl.semaphore_signal(bar, inc=1, device_id=device(*steps(i), core), device_id_type=MESH)
        return carry

    nxt, prv = lax.rem(me + 1, DEVICES), lax.rem(me + DEVICES - 1, DEVICES)
    line = [lax.rem(n + d, NARROW) for d in range(1, NARROW)]
    far_plane = ((2, 2), (1, 2), (2, 1), (3, 2), (2, 3), (0, 2), (2, 0))
    near_plane = ((1, 1), (3, 3), (1, 3), (3, 1), (0, 1), (1, 0), (0, 3), (3, 0))
    peers = [
        lax.rem(z + dz, 4) * 4 + lax.rem(x + dx, 4) for dz, dx in far_plane + near_plane
    ]
    lax.fori_loop(1, 27, greet, 0)
    pl.semaphore_signal(bar, inc=1, device_id=device(0, 0, 0, 1 - c), device_id_type=MESH)
    for p in (nxt, prv):
        pl.semaphore_signal(bar, inc=1, device_id=(p // NARROW, p % NARROW), device_id_type=MESH)
    for p in peers[:7]:
        pl.semaphore_signal(bar, inc=1, device_id=(p, n), device_id_type=MESH)
    for core in range(2):
        pl.semaphore_signal(bar, inc=1, device_id=device(0, 0, 2, core), device_id_type=MESH)
    lo64, lo32 = lo_mask(64), lo_mask(32)
    to_rows(transfer, trows, 64, PARENTS)

    def remote(src, dst, ssem, rsem, dev):
        return pltpu.make_async_remote_copy(
            src_ref=src, dst_ref=dst, send_sem=ssem, recv_sem=rsem, device_id=dev, device_id_type=MESH
        )

    def parent_step(i, carry):
        zero = jnp.zeros((64, 128), BF16)
        for u in range(UNROLL):
            p = i * UNROLL + u
            at = 128 * u
            cols = pl.ds(pl.multiple_of(p * 128, 128), 128)
            b, q = basis[:, cols], q_ref[:, cols]
            bb = jnp.concatenate([jnp.where(lo64, b, zero), jnp.where(lo64, zero, b)], axis=0)
            bbd[p] = bb
            qq = jnp.concatenate([q, q], axis=0)
            leaf = mm(bb, qq, ((1,), (1,))).astype(BF16)
            x_ref[2 * p] = jnp.where(lo32, leaf[0:32], leaf[32:64])
            x_ref[2 * p + 1] = jnp.where(lo32, leaf[64:96], leaf[96:128])
            v[at : at + 128] = leaf.astype(F32)
            even, odd = v[pl.ds(at, 64, stride=2), :], v[pl.ds(at + 1, 64, stride=2), :]
            paired = jnp.where(lo64, even, odd).astype(BF16)
            a = trows[pl.ds(p, 64, stride=PARENTS + 1), :].astype(BF16)
            down_lhs[p] = a
            m = mm(a, paired, ((0,), (0,)))
            s = jnp.where(lo64, m[0:64], m[64:128])
            parent = (s + swap_halves(s)).astype(BF16)
            x_ref[LEAF_DEV + p] = jnp.where(lo32, parent[0:32], parent[32:64])
        return carry

    def started(copy):
        copy.start()
        return copy

    pl.semaphore_wait(bar, 64)
    first = [started(remote(mine, table.at[w, n], ls.at[i], lr.at[i], (w, p))) for i, p in enumerate(line)]
    halos = [
        started(
            remote(q_ref.at[:, pl.ds(3968, 128)], halo.at[0], hs.at[0], hr.at[0], (nxt // NARROW, nxt % NARROW))
        ),
        started(remote(q_ref.at[:, pl.ds(0, 128)], halo.at[1], hs.at[1], hr.at[1], (prv // NARROW, prv % NARROW))),
    ]
    table[w, n] = mine[...]
    quarter = PARENTS // UNROLL // 4
    lax.fori_loop(0, quarter, parent_step, 0)
    for k in first:
        k.wait_recv()
    second = [
        started(remote(table.at[w], table.at[w], ts.at[i], tr.at[i], (p, n))) for i, p in enumerate(peers)
    ]
    lax.fori_loop(quarter, 4 * quarter, parent_step, 0)

    def build(i, carry):
        xbd[i] = spread(x_ref[i])
        return carry

    lax.fori_loop(0, NODES, build, 0, unroll=2)
    lane = lax.broadcasted_iota(I32, (128, 128), 1)
    sub = lax.broadcasted_iota(I32, (128, 128), 0)
    listv[...] = jnp.zeros_like(listv)
    placev[...] = jnp.zeros_like(placev)
    for b in range(BLOCKS):
        own_row = mine[b : b + 1, :] // 128
        same = jnp.broadcast_to(own_row, (128, 128))
        again = jnp.where((same.T == same) & (sub < lane), 1, 0)
        placev[b : b + 1, :] = own_row * CAP + 2 * b + jnp.max(again, axis=0, keepdims=True)
    place_copy = started(pltpu.make_async_copy(placev, place, ps.at[0]))
    for k in second:
        k.wait_recv()
    tables = table[...].reshape(DEVICES, TROWS, 128)
    for b in range(BLOCKS):
        t = tables[:, b, :].T
        named = (t // 128) == me
        code = sub * 128 + t % 128
        lowest = jnp.min(jnp.where(named, code, 128 * 128), axis=0, keepdims=True)
        highest = jnp.max(jnp.where(named, code, 0), axis=0, keepdims=True)
        listv[2 * b : 2 * b + 1, :] = lowest % 128
        listv[2 * b + 1 : 2 * b + 2, :] = highest % 128
    list_copy = started(pltpu.make_async_copy(listv, lists, ps.at[1]))
    list_copy.wait()
    place_copy.wait()

    def fill(r, carry):
        for s in range(CAP):
            send[r * CAP + s] = x_ref[jnp.minimum(lists[s, r], NODES - 1)]
        return carry

    lax.fori_loop(0, DEVICES, fill, 0)

    def relayed(act):
        base = 0
        for level, subsets in enumerate(SUBSETS):
            others = (9, 3, 1)[level]

            def body(i, carry, subsets=subsets, base=base, level=level):
                for core in range(2):
                    for h in range(2):
                        for k, axes in enumerate(subsets):
                            val = [i % 3, i // 3]
                            off = {}
                            for axis in "zxy":
                                if axis in axes:
                                    off[axis] = 2
                                else:
                                    a = val.pop(0)
                                    off[axis] = a + a // 2
                            hop = (1, 3)[h]
                            one = {axis: (hop if axis in axes else 0) for axis in "zxy"}
                            slot = base + ((i * len(subsets) + k) * 2 + core) * 2 + h
                            act(off, one, core, h, slot)
                return carry

            lax.fori_loop(0, others, body, 0)
            base += others * len(subsets) * 4

    def leg1(off, one, core, h, slot):
        tw, tn = device(off["z"], off["x"], off["y"], core)
        remote(
            send.at[pl.ds((tw * NARROW + tn) * CAP + h * HALF, HALF)],
            relay.at[pl.ds(slot * HALF, HALF)],
            s1,
            r1,
            device(one["z"], one["x"], one["y"], c),
        ).start()

    def leg2(off, one, core, h, slot):
        sw, sn = device(4 - one["z"], 4 - one["x"], 4 - one["y"], c)
        rest = {axis: off[axis] - one[axis] + 4 for axis in "zxy"}
        remote(
            relay.at[pl.ds(slot * HALF, HALF)],
            recv.at[pl.ds((sw * NARROW + sn) * CAP + h * HALF, HALF)],
            s2,
            r2,
            device(rest["z"], rest["x"], rest["y"], core),
        ).start()

    def direct(i, carry):
        j = lax.rem(i * 10, 27)
        dz, dx, dy = steps(j)
        for core in range(2):
            tw, tn = device(dz, dx, dy, core)
            remote(
                send.at[pl.ds((tw * NARROW + tn) * CAP, CAP)],
                recv.at[pl.ds(me * CAP, CAP)],
                s2,
                r2,
                (tw, tn),
            ).start()
        return carry

    relayed(leg1)
    lax.fori_loop(1, 27, direct, 0)
    tw, tn = device(0, 0, 0, 1 - c)
    remote(
        send.at[pl.ds((tw * NARROW + tn) * CAP, CAP)], recv.at[pl.ds(me * CAP, CAP)], s2, r2, (tw, tn)
    ).start()
    own = pltpu.make_async_copy(send.at[pl.ds(me * CAP, CAP)], recv.at[pl.ds(me * CAP, CAP)], dsem)
    own.start()

    def compute(g):
        if g + 1 < blocks:
            load(g + 1).start()
        load(g).wait()
        to_rows(cbuf.at[g % 2], rows, tiles, ROWS)
        offset = 0 if g * ROWS < LEAF_DEV else LEAF_DEV

        def node(i, carry):
            acc = jnp.zeros((32, 128), F32)
            row = g * ROWS + i
            a = rows[pl.ds(i, tiles, stride=ROWS + 1), :].astype(BF16)
            for k in range(K_FAR):
                at = 32 * (K_LOCAL + k)
                far_lhs[row, :, 128 * k : 128 * k + 128] = a[at : at + 32]
            for k in range(0, K_LOCAL, 2):
                lhs = jnp.concatenate([a[32 * k : 32 * k + 32], a[32 * k + 32 : 32 * k + 64]], axis=1)
                rhs = jnp.concatenate(
                    [xbd[slots[k, row] + offset], xbd[slots[k + 1, row] + offset]], axis=0
                )
                acc = acc + mm(lhs, rhs)
            coupled[row] = acc
            return carry

        lax.fori_loop(0, ROWS, node, 0, unroll=2)

    def build_near():
        eye = (
            lax.broadcasted_iota(I32, (128, 128), 0) == lax.broadcasted_iota(I32, (128, 128), 1)
        ).astype(BF16)

        def put(i, q):
            t = mm(eye, jnp.concatenate([q, q], axis=0), ((1,), (1,))).astype(BF16)
            zero = jnp.zeros((64, 128), BF16)
            for b in range(2):
                d = t[64 * b : 64 * b + 64]
                qbd[2 * i + b] = jnp.concatenate(
                    [jnp.where(lo64, d, zero), jnp.where(lo64, zero, d)], axis=0
                )

        for k in halos:
            k.wait_recv()
        put(0, jnp.where(me > 0, halo[0], jnp.zeros_like(halo[0])))
        put(PARENTS + 1, jnp.where(me < DEVICES - 1, halo[1], jnp.zeros_like(halo[1])))

        def build_q(i, carry):
            put(i + 1, q_ref[:, pl.ds(pl.multiple_of(i * 128, 128), 128)])
            return carry

        lax.fori_loop(0, PARENTS, build_q, 0)
        near_copy.wait()

    def compute_near(g):
        to_rows(nbuf.at[pl.ds(g * ROWS, ROWS)], nrows, 160, ROWS)

        def pair(i, carry):
            for u in range(2):
                p = 2 * i + u
                for b in range(2):
                    a = nrows[pl.ds(2 * p + b, 160, stride=ROWS + 1), :].astype(BF16)
                    acc = jnp.zeros((32, 128), F32)
                    for t in range(5):
                        acc = acc + mm(a[32 * t : 32 * t + 32], qbd[g * ROWS + 2 * p + b + t])
                    unpair(v, 128 * u + 64 * b, acc)
                out[:, pl.ds(pl.multiple_of(g * (ROWS * 64) + p * 128, 128), 128)] = v[
                    128 * u : 128 * u + 128
                ].T[0:64]
            return carry

        lax.fori_loop(0, ROWS // 4, pair, 0)

    def far_node(n, carry):
        acc = coupled[n]
        for k in range(0, K_FAR, 2):
            first = recv[place[n // 32, (n % 32) * K_FAR + k]]
            second = recv[place[n // 32, (n % 32) * K_FAR + k + 1]]
            rhs = jnp.concatenate([spread(first), spread(second)], axis=0)
            acc = acc + mm(far_lhs[n, :, 128 * k : 128 * k + 256], rhs)
        coupled[n] = acc
        return carry

    def way_down(i, carry):
        for u in range(UNROLL):
            p = i * UNROLL + u
            at = 128 * u
            unpair(v, at, coupled[LEAF_DEV + p])
            d = v[at : at + 64].astype(BF16)
            zero = jnp.zeros_like(d)
            down = jnp.concatenate([jnp.where(lo64, d, zero), jnp.where(lo64, zero, d)], axis=0)
            add = mm(down_lhs[p], down)
            unpair(v, at, coupled[2 * p] + add[0:32])
            unpair(v, at + 64, coupled[2 * p + 1] + add[32:64])
            leaf_down = v[at : at + 128].astype(BF16)
            cols = pl.ds(pl.multiple_of(p * 128, 128), 128)
            out[:, cols] = out[:, cols] + mm(leaf_down, bbd[p], ((0,), (0,)))[0:64]
        return carry

    compute(0)
    compute(1)
    compute(2)
    build_near()
    pltpu.make_async_copy(relay, relay, r1).wait()
    relayed(leg2)
    compute(3)
    compute(4)
    compute(5)
    for g in range(LEAF_DEV // ROWS):
        compute_near(g)
    own.wait()
    part = recv.at[pl.ds(0, 127 * CAP)]
    pltpu.make_async_copy(part, part, r2).wait()
    lax.fori_loop(0, NODES, far_node, 0, unroll=4)
    lax.fori_loop(0, PARENTS // UNROLL, way_down, 0)
    pltpu.make_async_copy(relay, relay, s1).wait()
    pltpu.make_async_copy(part, part, s2).wait()
    for k in first + second + halos:
        k.wait_send()


def product(slots, mine, coupling, near, charges, transfer, basis):
    vm = pl.BlockSpec(memory_space=pltpu.VMEM)
    sm = pl.BlockSpec(memory_space=pltpu.SMEM)
    hbm = pl.BlockSpec(memory_space=pl.ANY)
    return pl.pallas_call(
        product_kernel,
        out_shape=jax.ShapeDtypeStruct((64, 4096), F32),
        in_specs=[sm, vm, hbm, hbm, vm, vm, vm],
        out_specs=vm,
        scratch_shapes=[
            pltpu.VMEM((NODES, 32, 128), BF16),
            pltpu.VMEM((WIDE, NARROW, TROWS, 128), I32),
            pltpu.VMEM((2, 64, 128), BF16),
            pltpu.VMEM((8, 128), I32),
            pltpu.VMEM((8, 128), I32),
            pltpu.SMEM((8, 128), I32),
            pltpu.SMEM((8, 128), I32),
            pltpu.VMEM((DEVICES * CAP, 32, 128), BF16),
            pltpu.VMEM((NODES, 32, 128), F32),
            pltpu.VMEM((DEVICES * CAP, 32, 128), BF16),
            pltpu.VMEM((148 * HALF, 32, 128), BF16),
            pltpu.VMEM((2, ROWS, 4096 * (K_LOCAL + K_FAR)), BF16),
            pltpu.VMEM((LEAF_DEV, 20480), BF16),
            pltpu.VMEM((NODES, 128, 128), BF16),
            pltpu.VMEM((LEAF_DEV + 4, 128, 128), BF16),
            pltpu.VMEM((32 * (K_LOCAL + K_FAR) * (ROWS + 1), 128), F32),
            pltpu.VMEM((160 * (ROWS + 1), 128), F32),
            pltpu.VMEM((64 * (PARENTS + 1), 128), F32),
            pltpu.VMEM((NODES, 32, 128 * K_FAR), BF16),
            pltpu.VMEM((PARENTS, 64, 128), BF16),
            pltpu.VMEM((PARENTS, 128, 128), BF16),
            pltpu.VMEM((UNROLL * 128, 128), F32),
            pltpu.SemaphoreType.DMA,
            pltpu.SemaphoreType.DMA,
            pltpu.SemaphoreType.DMA,
            pltpu.SemaphoreType.DMA,
            pltpu.SemaphoreType.DMA,
            pltpu.SemaphoreType.DMA((2,)),
            pltpu.SemaphoreType.DMA,
            pltpu.SemaphoreType.DMA((7,)),
            pltpu.SemaphoreType.DMA((7,)),
            pltpu.SemaphoreType.DMA((15,)),
            pltpu.SemaphoreType.DMA((15,)),
            pltpu.SemaphoreType.DMA((2,)),
            pltpu.SemaphoreType.DMA((2,)),
            pltpu.SemaphoreType.DMA((2,)),
        ],
        compiler_params=pltpu.CompilerParams(
            collective_id=0, has_side_effects=True, vmem_limit_bytes=VMEM_LIMIT
        ),
        name="product",
    )(slots, mine, coupling, near, charges, transfer, basis)


def shards(charges, basis, transfer, coupling, near_blocks, local_slot, owner, far_slot):
    offset = jnp.where(jnp.arange(NODES) < LEAF_DEV, 0, LEAF_DEV).astype(I32)[:, None]
    entry = (owner * 128 + far_slot + offset).reshape(3, 128)
    mine = jnp.pad(entry, ((0, TROWS - 3), (0, 0)))
    return product(local_slot.T, mine, coupling, near_blocks, charges, transfer, basis)


def solution(mesh):
    cols, rows = P(None, ("wide", "narrow")), P(("wide", "narrow"), None)
    return jax.shard_map(
        shards,
        mesh=mesh,
        in_specs=(cols, cols, rows, rows, rows, rows, rows, rows),
        out_specs=cols,
        check_vma=False,
    )
```

```python
import functools

import jax
import jax.numpy as jnp
from jax import lax
from jax.experimental import pallas as pl
from jax.experimental.pallas import tpu as pltpu
from jax.sharding import PartitionSpec as P

MESH = pl.DeviceIdType.MESH
F32, BF16, I32 = jnp.float32, jnp.bfloat16, jnp.int32

WIDE, NARROW = 16, 8
LEAF_DEV, PARENTS, NODES = 64, 32, 96
K_LOCAL, K_FAR = 20, 4
DEVICES = WIDE * NARROW
BLOCKS = 3
TROWS = 4
UNROLL = 4
CAP = 6
PART = (4, 2)
VMEM_LIMIT = 56 << 20


def lo_mask(rows):
    return lax.broadcasted_iota(I32, (rows, 128), 1) < 64


def swap_halves(x):
    return jnp.concatenate([x[:, 64:], x[:, :64]], axis=1)


def mm(a, b, dims=((1,), (0,))):
    return lax.dot_general(a, b, (dims, ((), ())), preferred_element_type=F32)


def spread(tile):
    lo = lo_mask(32)
    zero = jnp.zeros_like(tile)
    turned = swap_halves(tile)
    return jnp.concatenate(
        [
            jnp.where(lo, tile, zero),
            jnp.where(lo, turned, zero),
            jnp.where(lo, zero, turned),
            jnp.where(lo, zero, tile),
        ],
        axis=0,
    )


def unpair(ref, start, packed):
    lo = lo_mask(32)
    turned = swap_halves(packed)
    ref[pl.ds(start, 32, stride=2), :] = jnp.where(lo, packed, turned)
    ref[pl.ds(start + 1, 32, stride=2), :] = jnp.where(lo, turned, packed)


def to_rows(src, dst, tiles, rows):
    def step(g, c):
        for u in range(8):
            t = g * 8 + u
            dst[pl.ds(t * (rows + 1), rows), :] = src[
                :, pl.ds(pl.multiple_of(t * 128, 128), 128)
            ].astype(F32)
        return c

    lax.fori_loop(0, tiles // 8, step, 0)


ROWS = 16
SUBSETS = ("z", "x", "y"), ("zx", "zy", "xy"), ("zxy",)


def product_kernel(
    slots, mine, coupling, near, q_ref, transfer, basis, out,
    x_ref, table, halo, listv, placev, lists, place, recv0, recv1, coupled, send0, send1, relay0, relay1, cbuf, nbuf, xbd, qbd, rows, nrows, trows, far_lhs, down_lhs, bbd,
    v, s1, r1, s2, r2, dsem, csem, nsem, ls, lr, ts, tr, hs, hr, ps,
):
    w, n = lax.axis_index("wide"), lax.axis_index("narrow")
    me = w * NARROW + n
    z, x, y, c = w // 4, w % 4, n // 2, n % 2
    tiles = 32 * (K_LOCAL + K_FAR)
    blocks = NODES // ROWS

    def load(g):
        return pltpu.make_async_copy(
            coupling.at[pl.ds(g * ROWS, ROWS)], cbuf.at[g % 2], csem.at[g % 2]
        )

    load(0).start()
    near_copy = pltpu.make_async_copy(near, nbuf, nsem)
    near_copy.start()

    def device(dz, dx, dy, core):
        return (
            lax.rem(z + dz, 4) * 4 + lax.rem(x + dx, 4),
            lax.rem(y + dy, 4) * 2 + core,
        )

    bar = pltpu.get_barrier_semaphore()

    def steps(i):
        a, b, d = i // 9, (i // 3) % 3, i % 3
        return a + a // 2, b + b // 2, d + d // 2

    def greet(i, carry):
        for core in range(2):
            pl.semaphore_signal(bar, inc=1, device_id=device(*steps(i), core), device_id_type=MESH)
        return carry

    nxt, prv = lax.rem(me + 1, DEVICES), lax.rem(me + DEVICES - 1, DEVICES)
    line = [lax.rem(n + d, NARROW) for d in range(1, NARROW)]
    far_plane = ((2, 2), (1, 2), (2, 1), (3, 2), (2, 3), (0, 2), (2, 0))
    near_plane = ((1, 1), (3, 3), (1, 3), (3, 1), (0, 1), (1, 0), (0, 3), (3, 0))
    peers = [
        lax.rem(z + dz, 4) * 4 + lax.rem(x + dx, 4) for dz, dx in far_plane + near_plane
    ]
    lax.fori_loop(1, 27, greet, 0)
    pl.semaphore_signal(bar, inc=1, device_id=device(0, 0, 0, 1 - c), device_id_type=MESH)
    for p in (nxt, prv):
        pl.semaphore_signal(bar, inc=1, device_id=(p // NARROW, p % NARROW), device_id_type=MESH)
    for p in peers[:7]:
        pl.semaphore_signal(bar, inc=1, device_id=(p, n), device_id_type=MESH)
    for core in range(2):
        pl.semaphore_signal(bar, inc=1, device_id=device(0, 0, 2, core), device_id_type=MESH)
    lo64, lo32 = lo_mask(64), lo_mask(32)
    to_rows(transfer, trows, 64, PARENTS)

    def remote(src, dst, ssem, rsem, dev):
        return pltpu.make_async_remote_copy(
            src_ref=src, dst_ref=dst, send_sem=ssem, recv_sem=rsem, device_id=dev, device_id_type=MESH
        )

    def parent_step(i, carry):
        zero = jnp.zeros((64, 128), BF16)
        for u in range(UNROLL):
            p = i * UNROLL + u
            at = 128 * u
            cols = pl.ds(pl.multiple_of(p * 128, 128), 128)
            b, q = basis[:, cols], q_ref[:, cols]
            bb = jnp.concatenate([jnp.where(lo64, b, zero), jnp.where(lo64, zero, b)], axis=0)
            bbd[p] = bb
            qq = jnp.concatenate([q, q], axis=0)
            leaf = mm(bb, qq, ((1,), (1,))).astype(BF16)
            x_ref[2 * p] = jnp.where(lo32, leaf[0:32], leaf[32:64])
            x_ref[2 * p + 1] = jnp.where(lo32, leaf[64:96], leaf[96:128])
            v[at : at + 128] = leaf.astype(F32)
            even, odd = v[pl.ds(at, 64, stride=2), :], v[pl.ds(at + 1, 64, stride=2), :]
            paired = jnp.where(lo64, even, odd).astype(BF16)
            a = trows[pl.ds(p, 64, stride=PARENTS + 1), :].astype(BF16)
            down_lhs[p] = a
            m = mm(a, paired, ((0,), (0,)))
            s = jnp.where(lo64, m[0:64], m[64:128])
            parent = (s + swap_halves(s)).astype(BF16)
            x_ref[LEAF_DEV + p] = jnp.where(lo32, parent[0:32], parent[32:64])
        return carry

    def started(copy):
        copy.start()
        return copy

    pl.semaphore_wait(bar, 64)
    first = [started(remote(mine, table.at[w, n], ls.at[i], lr.at[i], (w, p))) for i, p in enumerate(line)]
    halos = [
        started(
            remote(q_ref.at[:, pl.ds(3968, 128)], halo.at[0], hs.at[0], hr.at[0], (nxt // NARROW, nxt % NARROW))
        ),
        started(remote(q_ref.at[:, pl.ds(0, 128)], halo.at[1], hs.at[1], hr.at[1], (prv // NARROW, prv % NARROW))),
    ]
    table[w, n] = mine[...]
    quarter = PARENTS // UNROLL // 4
    lax.fori_loop(0, quarter, parent_step, 0)
    for k in first:
        k.wait_recv()
    second = [
        started(remote(table.at[w], table.at[w], ts.at[i], tr.at[i], (p, n))) for i, p in enumerate(peers)
    ]
    lax.fori_loop(quarter, 4 * quarter, parent_step, 0)

    def build(i, carry):
        xbd[i] = spread(x_ref[i])
        return carry

    lax.fori_loop(0, NODES, build, 0, unroll=2)
    lane = lax.broadcasted_iota(I32, (128, 128), 1)
    sub = lax.broadcasted_iota(I32, (128, 128), 0)
    listv[...] = jnp.zeros_like(listv)
    placev[...] = jnp.zeros_like(placev)
    for b in range(BLOCKS):
        own_row = mine[b : b + 1, :] // 128
        same = jnp.broadcast_to(own_row, (128, 128))
        again = jnp.where((same.T == same) & (sub < lane), 1, 0)
        placev[b : b + 1, :] = own_row * PART[b % 2] + (2, 0, 0)[b] + jnp.max(again, axis=0, keepdims=True)
    place_copy = started(pltpu.make_async_copy(placev, place, ps.at[0]))
    for k in second:
        k.wait_recv()
    tables = table[...].reshape(DEVICES, TROWS, 128)
    for b in range(BLOCKS):
        t = tables[:, b, :].T
        named = (t // 128) == me
        code = sub * 128 + t % 128
        lowest = jnp.min(jnp.where(named, code, 128 * 128), axis=0, keepdims=True)
        highest = jnp.max(jnp.where(named, code, 0), axis=0, keepdims=True)
        listv[2 * b : 2 * b + 1, :] = lowest % 128
        listv[2 * b + 1 : 2 * b + 2, :] = highest % 128
    list_copy = started(pltpu.make_async_copy(listv, lists, ps.at[1]))
    list_copy.wait()
    place_copy.wait()

    def fill(r, carry):
        for s, row in enumerate((4, 5, 0, 1)):
            send0[r * PART[0] + s] = x_ref[jnp.minimum(lists[row, r], NODES - 1)]
        for s, row in enumerate((2, 3)):
            send1[r * PART[1] + s] = x_ref[jnp.minimum(lists[row, r], NODES - 1)]
        return carry

    lax.fori_loop(0, DEVICES, fill, 0)

    def relayed(act):
        base = 0
        for level, subsets in enumerate(SUBSETS):
            others = (9, 3, 1)[level]

            def body(i, carry, subsets=subsets, base=base, level=level):
                for core in range(2):
                    for h in range(2):
                        for k, axes in enumerate(subsets):
                            val = [i % 3, i // 3]
                            off = {}
                            for axis in "zxy":
                                if axis in axes:
                                    off[axis] = 2
                                else:
                                    a = val.pop(0)
                                    off[axis] = a + a // 2
                            hop = (1, 3)[h]
                            one = {axis: (hop if axis in axes else 0) for axis in "zxy"}
                            slot = base + ((i * len(subsets) + k) * 2 + core) * 2 + h
                            act(off, one, core, h, slot)
                return carry

            lax.fori_loop(0, others, body, 0)
            base += others * len(subsets) * 4

    send, relay, recv = (send0, send1), (relay0, relay1), (recv0, recv1)

    def leg1(q, off, one, core, h, slot):
        half = PART[q] // 2
        tw, tn = device(off["z"], off["x"], off["y"], core)
        remote(
            send[q].at[pl.ds((tw * NARROW + tn) * PART[q] + h * half, half)],
            relay[q].at[pl.ds(slot * half, half)],
            s1.at[q],
            r1.at[q],
            device(one["z"], one["x"], one["y"], c),
        ).start()

    def leg2(q, off, one, core, h, slot):
        half = PART[q] // 2
        sw, sn = device(4 - one["z"], 4 - one["x"], 4 - one["y"], c)
        rest = {axis: off[axis] - one[axis] + 4 for axis in "zxy"}
        remote(
            relay[q].at[pl.ds(slot * half, half)],
            recv[q].at[pl.ds((sw * NARROW + sn) * PART[q] + h * half, half)],
            s2.at[q],
            r2.at[q],
            device(rest["z"], rest["x"], rest["y"], core),
        ).start()

    def straight(q, tw, tn):
        remote(
            send[q].at[pl.ds((tw * NARROW + tn) * PART[q], PART[q])],
            recv[q].at[pl.ds(me * PART[q], PART[q])],
            s2.at[q],
            r2.at[q],
            (tw, tn),
        ).start()

    def directs(q):
        def direct(i, carry):
            j = lax.rem(i * 10, 27)
            for core in range(2):
                straight(q, *device(*steps(j), core))
            return carry

        lax.fori_loop(1, 27, direct, 0)
        straight(q, *device(0, 0, 0, 1 - c))

    def forward(q):
        pltpu.make_async_copy(relay[q], relay[q], r1.at[q]).wait()
        relayed(functools.partial(leg2, q))

    relayed(functools.partial(leg1, 0))
    relayed(functools.partial(leg1, 1))
    directs(0)
    own = [
        started(
            pltpu.make_async_copy(
                send[q].at[pl.ds(me * PART[q], PART[q])], recv[q].at[pl.ds(me * PART[q], PART[q])], dsem.at[q]
            )
        )
        for q in range(2)
    ]

    def compute(g):
        if g + 1 < blocks:
            load(g + 1).start()
        load(g).wait()
        to_rows(cbuf.at[g % 2], rows, tiles, ROWS)
        offset = 0 if g * ROWS < LEAF_DEV else LEAF_DEV

        def node(i, carry):
            acc = jnp.zeros((32, 128), F32)
            row = g * ROWS + i
            a = rows[pl.ds(i, tiles, stride=ROWS + 1), :].astype(BF16)
            for k in range(K_FAR):
                at = 32 * (K_LOCAL + k)
                far_lhs[row, :, 128 * k : 128 * k + 128] = a[at : at + 32]
            for k in range(0, K_LOCAL, 2):
                lhs = jnp.concatenate([a[32 * k : 32 * k + 32], a[32 * k + 32 : 32 * k + 64]], axis=1)
                rhs = jnp.concatenate(
                    [xbd[slots[k, row] + offset], xbd[slots[k + 1, row] + offset]], axis=0
                )
                acc = acc + mm(lhs, rhs)
            coupled[row] = acc
            return carry

        lax.fori_loop(0, ROWS, node, 0, unroll=2)

    def build_near():
        eye = (
            lax.broadcasted_iota(I32, (128, 128), 0) == lax.broadcasted_iota(I32, (128, 128), 1)
        ).astype(BF16)

        def put(i, q):
            t = mm(eye, jnp.concatenate([q, q], axis=0), ((1,), (1,))).astype(BF16)
            zero = jnp.zeros((64, 128), BF16)
            for b in range(2):
                d = t[64 * b : 64 * b + 64]
                qbd[2 * i + b] = jnp.concatenate(
                    [jnp.where(lo64, d, zero), jnp.where(lo64, zero, d)], axis=0
                )

        for k in halos:
            k.wait_recv()
        put(0, jnp.where(me > 0, halo[0], jnp.zeros_like(halo[0])))
        put(PARENTS + 1, jnp.where(me < DEVICES - 1, halo[1], jnp.zeros_like(halo[1])))

        def build_q(i, carry):
            put(i + 1, q_ref[:, pl.ds(pl.multiple_of(i * 128, 128), 128)])
            return carry

        lax.fori_loop(0, PARENTS, build_q, 0)
        near_copy.wait()

    def compute_near(g):
        to_rows(nbuf.at[pl.ds(g * ROWS, ROWS)], nrows, 160, ROWS)

        def pair(i, carry):
            for u in range(2):
                p = 2 * i + u
                for b in range(2):
                    a = nrows[pl.ds(2 * p + b, 160, stride=ROWS + 1), :].astype(BF16)
                    acc = jnp.zeros((32, 128), F32)
                    for t in range(5):
                        acc = acc + mm(a[32 * t : 32 * t + 32], qbd[g * ROWS + 2 * p + b + t])
                    unpair(v, 128 * u + 64 * b, acc)
                out[:, pl.ds(pl.multiple_of(g * (ROWS * 64) + p * 128, 128), 128)] = v[
                    128 * u : 128 * u + 128
                ].T[0:64]
            return carry

        lax.fori_loop(0, ROWS // 4, pair, 0)

    def far_node(q, n, carry):
        acc = coupled[n]
        for k in range(0, K_FAR, 2):
            first = recv[q][place[n // 32, (n % 32) * K_FAR + k]]
            second = recv[q][place[n // 32, (n % 32) * K_FAR + k + 1]]
            rhs = jnp.concatenate([spread(first), spread(second)], axis=0)
            acc = acc + mm(far_lhs[n, :, 128 * k : 128 * k + 256], rhs)
        coupled[n] = acc
        return carry

    def way_down(i, carry):
        for u in range(UNROLL):
            p = i * UNROLL + u
            at = 128 * u
            unpair(v, at, coupled[LEAF_DEV + p])
            d = v[at : at + 64].astype(BF16)
            zero = jnp.zeros_like(d)
            down = jnp.concatenate([jnp.where(lo64, d, zero), jnp.where(lo64, zero, d)], axis=0)
            add = mm(down_lhs[p], down)
            unpair(v, at, coupled[2 * p] + add[0:32])
            unpair(v, at + 64, coupled[2 * p + 1] + add[32:64])
            leaf_down = v[at : at + 128].astype(BF16)
            cols = pl.ds(pl.multiple_of(p * 128, 128), 128)
            out[:, cols] = out[:, cols] + mm(leaf_down, bbd[p], ((0,), (0,)))[0:64]
        return carry

    compute(0)
    compute(1)
    compute(2)
    forward(0)
    directs(1)
    build_near()
    compute(3)
    forward(1)
    compute(4)
    compute(5)
    for g in range(LEAF_DEV // ROWS):
        compute_near(g)
    groups = PARENTS // UNROLL // 2
    for q, spans in enumerate((((LEAF_DEV, NODES), (0, 32)), ((32, LEAF_DEV),))):
        own[q].wait()
        arrived = recv[q].at[pl.ds(0, 127 * PART[q])]
        pltpu.make_async_copy(arrived, arrived, r2.at[q]).wait()
        for start, stop in spans:
            lax.fori_loop(start, stop, functools.partial(far_node, q), 0, unroll=4)
        lax.fori_loop(q * groups, (q + 1) * groups, way_down, 0)
    for q in range(2):
        pltpu.make_async_copy(relay[q], relay[q], s1.at[q]).wait()
        sent = send[q].at[pl.ds(0, 127 * PART[q])]
        pltpu.make_async_copy(sent, sent, s2.at[q]).wait()
    for k in first + second + halos:
        k.wait_send()


def product(slots, mine, coupling, near, charges, transfer, basis):
    vm = pl.BlockSpec(memory_space=pltpu.VMEM)
    sm = pl.BlockSpec(memory_space=pltpu.SMEM)
    hbm = pl.BlockSpec(memory_space=pl.ANY)
    return pl.pallas_call(
        product_kernel,
        out_shape=jax.ShapeDtypeStruct((64, 4096), F32),
        in_specs=[sm, vm, hbm, hbm, vm, vm, vm],
        out_specs=vm,
        scratch_shapes=[
            pltpu.VMEM((NODES, 32, 128), BF16),
            pltpu.VMEM((WIDE, NARROW, TROWS, 128), I32),
            pltpu.VMEM((2, 64, 128), BF16),
            pltpu.VMEM((8, 128), I32),
            pltpu.VMEM((8, 128), I32),
            pltpu.SMEM((8, 128), I32),
            pltpu.SMEM((8, 128), I32),
            pltpu.VMEM((DEVICES * PART[0], 32, 128), BF16),
            pltpu.VMEM((DEVICES * PART[1], 32, 128), BF16),
            pltpu.VMEM((NODES, 32, 128), F32),
            pltpu.VMEM((DEVICES * PART[0], 32, 128), BF16),
            pltpu.VMEM((DEVICES * PART[1], 32, 128), BF16),
            pltpu.VMEM((148 * PART[0] // 2, 32, 128), BF16),
            pltpu.VMEM((148 * PART[1] // 2, 32, 128), BF16),
            pltpu.VMEM((2, ROWS, 4096 * (K_LOCAL + K_FAR)), BF16),
            pltpu.VMEM((LEAF_DEV, 20480), BF16),
            pltpu.VMEM((NODES, 128, 128), BF16),
            pltpu.VMEM((LEAF_DEV + 4, 128, 128), BF16),
            pltpu.VMEM((32 * (K_LOCAL + K_FAR) * (ROWS + 1), 128), F32),
            pltpu.VMEM((160 * (ROWS + 1), 128), F32),
            pltpu.VMEM((64 * (PARENTS + 1), 128), F32),
            pltpu.VMEM((NODES, 32, 128 * K_FAR), BF16),
            pltpu.VMEM((PARENTS, 64, 128), BF16),
            pltpu.VMEM((PARENTS, 128, 128), BF16),
            pltpu.VMEM((UNROLL * 128, 128), F32),
            pltpu.SemaphoreType.DMA((2,)),
            pltpu.SemaphoreType.DMA((2,)),
            pltpu.SemaphoreType.DMA((2,)),
            pltpu.SemaphoreType.DMA((2,)),
            pltpu.SemaphoreType.DMA((2,)),
            pltpu.SemaphoreType.DMA((2,)),
            pltpu.SemaphoreType.DMA,
            pltpu.SemaphoreType.DMA((7,)),
            pltpu.SemaphoreType.DMA((7,)),
            pltpu.SemaphoreType.DMA((15,)),
            pltpu.SemaphoreType.DMA((15,)),
            pltpu.SemaphoreType.DMA((2,)),
            pltpu.SemaphoreType.DMA((2,)),
            pltpu.SemaphoreType.DMA((2,)),
        ],
        compiler_params=pltpu.CompilerParams(
            collective_id=0, has_side_effects=True, vmem_limit_bytes=VMEM_LIMIT
        ),
        name="product",
    )(slots, mine, coupling, near, charges, transfer, basis)


def shards(charges, basis, transfer, coupling, near_blocks, local_slot, owner, far_slot):
    offset = jnp.where(jnp.arange(NODES) < LEAF_DEV, 0, LEAF_DEV).astype(I32)[:, None]
    entry = (owner * 128 + far_slot + offset).reshape(3, 128)
    mine = jnp.pad(entry, ((0, TROWS - 3), (0, 0)))
    return product(local_slot.T, mine, coupling, near_blocks, charges, transfer, basis)


def solution(mesh):
    cols, rows = P(None, ("wide", "narrow")), P(("wide", "narrow"), None)
    return jax.shard_map(
        shards,
        mesh=mesh,
        in_specs=(cols, cols, rows, rows, rows, rows, rows, rows),
        out_specs=cols,
        check_vma=False,
    )
```
